32 devices in a mesh: gx: 4 (over z), gy: 4 (over y, x), gz: 2 (over core).
Axes of the slice: x: 2, y: 2, z: 4, core: 2. Of those that a mesh axis runs over, the one named last changes fastest.
Arguments:
- tokens: bfloat16 [4, 2048, 2048], P('gx', ('gy', 'gz')), may hold values from -6 to 6
- lengths: int32 [4, 6], P('gx'), may hold values from 60 to 800, as said below
- ln1_gain: bfloat16 [2048], replicated, may hold values from 0.5 to 1.5
- ln1_bias: bfloat16 [2048], replicated, may hold values from -1 to 1
- qkv_weight: bfloat16 [2048, 3, 2048], P('gx', None, ('gy', 'gz')), may hold values from -0.125 to 0.125
- qkv_bias: bfloat16 [3, 2048], P(None, ('gy', 'gz')), may hold values from -3 to 3
- out_weight: bfloat16 [2048, 2048], P('gx', ('gy', 'gz')), may hold values from -1 to 1
- ln2_gain: bfloat16 [2048], replicated, may hold values from 0.5 to 1.5
- ln2_bias: bfloat16 [2048], replicated, may hold values from -1 to 1
- gate_up_weight: bfloat16 [2048, 2, 5632], P('gx', None, ('gy', 'gz')), may hold values from -0.125 to 0.125
- down_weight: bfloat16 [2048, 5632], P('gx', ('gy', 'gz')), may hold values from -0.078125 to 0.078125
- cotangent: bfloat16 [4, 2048, 2048], P('gx', ('gy', 'gz')), may hold values from -6 to 6
Outputs:
- activations: bfloat16 [4, 2048, 2048], P('gx', ('gy', 'gz'))
- input_grad: bfloat16 [4, 2048, 2048], P('gx', ('gy', 'gz'))
- ln1_gain_grad: float32 [2048], replicated
- ln1_bias_grad: float32 [2048], replicated
- qkv_weight_grad: float32 [2048, 3, 2048], P('gx', None, ('gy', 'gz'))
- qkv_bias_grad: float32 [3, 2048], P(None, ('gy', 'gz'))
- out_weight_grad: float32 [2048, 2048], P('gx', ('gy', 'gz'))
- ln2_gain_grad: float32 [2048], replicated
- ln2_bias_grad: float32 [2048], replicated
- gate_up_grad: float32 [2048, 2, 5632], P('gx', None, ('gy', 'gz'))
- down_grad: float32 [2048, 5632], P('gx', ('gy', 'gz'))
The draws below stay inside these ranges and needn't reach their ends.
Inputs may be any that keep to these rules, and one draw needn't show every extreme that they name: Each sequence holds 6 documents in order, their lengths summing to 2048; every sequence has one document of exactly 800 tokens and one of exactly 60 tokens.
All inputs are finite; a program needn't handle non-finite values.
Results may differ from the reference program's by a relative error of at most 0.015.
Values may be sent and summed in bfloat16 or wider, within the bound.
No kernel may reach another device: no remote copies, remote signals or barrier semaphores. Data moves between devices by JAX's collectives and lax.ppermute only.
A program may use at most 320 MiB of HBM per device.

```python
import math
import jax
import jax.numpy as jnp
from jax import lax

D = 2048
HEADS = 32
HEAD_DIM = 64
ROT = 16
FF = 5632
LEN = 2048
DOCS = 6
NSEQ = 4
DOC_MAX = 800
DOC_MIN = 60


def draw_lengths(key, part):
    key = jax.random.fold_in(key, 7)
    share_key, order_key = jax.random.split(key, 2)
    shares = jax.random.randint(share_key, (NSEQ, 4), 200, 1001)
    extra_total = LEN - DOC_MAX - 5 * DOC_MIN
    extras = extra_total * shares // jnp.sum(shares, axis=1, keepdims=True)
    leading = extras[:, :3]
    closing = extra_total - jnp.sum(leading, axis=1, keepdims=True)
    others = DOC_MIN + jnp.concatenate([leading, closing], axis=1)
    base = jnp.concatenate([jnp.full((NSEQ, 1), DOC_MAX, jnp.int32), jnp.full((NSEQ, 1), DOC_MIN, jnp.int32), others.astype(jnp.int32)], axis=1)
    orders = jax.vmap(lambda one_key: jax.random.permutation(one_key, DOCS))(jax.random.split(order_key, NSEQ))
    return jnp.take_along_axis(base, orders.astype(jnp.int32), axis=1).astype(jnp.int32)


def steps_of(rng, extent, cuts, low, high):
    level, own = 1.0, jax.random.fold_in(rng, 6)
    for axis_at, blocks in cuts:
        heights = jnp.exp(jax.random.uniform(jax.random.fold_in(own, axis_at), (blocks,), jnp.float32, low / len(cuts), high / len(cuts)))
        level = level * jnp.repeat(heights, extent[axis_at] // blocks).reshape([-1 if axis == axis_at else 1 for axis in range(len(extent))])
    return level


def gaussian(own_key, shape, deviation, bound, cuts=(), kind=jnp.bfloat16):
    result = jax.random.normal(own_key, shape, jnp.float32) * deviation
    if len(cuts) > 0:
        result = steps_of(own_key, shape, cuts, -0.22, 0.18) * result
    return jnp.clip(result, min=-bound, max=bound).astype(kind)


def setup_inputs(seed: int = 0) -> dict:
    key_list = jax.random.split(jax.random.key(seed), 13)
    return {
        "tokens": gaussian(key_list[0], (NSEQ, LEN, D), 1.0, 6.0, ((0, 4), (1, 8))),
        "lengths": draw_lengths(jax.random.fold_in(key_list[12], 71), 0),
        "ln1_gain": jnp.clip(1.0 + 0.1 * jax.random.normal(key_list[2], (D,), jnp.float32), 0.5, 1.5).astype(jnp.bfloat16),
        "ln1_bias": gaussian(key_list[3], (D,), 0.2, 1.0),
        "qkv_weight": gaussian(key_list[4], (D, 3, D), D ** -0.5, 0.125, ((0, 4), (2, 8))),
        "qkv_bias": gaussian(key_list[5], (3, D), 0.5, 3.0, ((1, 8),)),
        "out_weight": gaussian(key_list[6], (D, D), (D // 64) ** -0.5, 1.0, ((0, 4), (1, 8))),
        "ln2_gain": jnp.clip(1.0 + 0.1 * jax.random.normal(key_list[7], (D,), jnp.float32), 0.5, 1.5).astype(jnp.bfloat16),
        "ln2_bias": gaussian(key_list[8], (D,), 0.2, 1.0),
        "gate_up_weight": gaussian(key_list[9], (D, 2, FF), D ** -0.5, 0.125, ((0, 4), (2, 8))),
        "down_weight": gaussian(key_list[10], (D, FF), FF ** -0.5, 0.078125, ((0, 4), (1, 8))),
        "cotangent": gaussian(key_list[11], (NSEQ, LEN, D), 1.0, 6.0, ((0, 4), (1, 8))),
    }


@jax.custom_vjp
def low(v):
    return lax.optimization_barrier(v.astype(jnp.bfloat16)).astype(jnp.float32)

@jax.custom_vjp
def low_back(v):
    return v

def low_keep(v):
    return (low(v), None)

def low_pass(kept, grad):
    return (grad,)

def back_keep(v):
    return (v, None)

def back_low(kept, grad):
    return (low(grad),)
low.defvjp(low_keep, low_pass)
low_back.defvjp(back_keep, back_low)

def layer_norm(values, norm_gain, norm_shift):
    average = lax.optimization_barrier(jnp.mean(values, axis=-1, keepdims=True))
    centered = values - average
    variance = lax.optimization_barrier(jnp.mean(centered * centered, axis=-1, keepdims=True))
    return centered * lax.rsqrt(variance + 1e-05) * norm_gain + norm_shift

def doc_tables(doc_lengths, seq_length):
    doc_ends = jnp.cumsum(doc_lengths).astype(jnp.int32)
    doc_starts = (doc_ends - doc_lengths).astype(jnp.int32)
    places = jnp.arange(seq_length, dtype=jnp.int32)
    segment = lax.optimization_barrier(jnp.sum((places[:, None] >= doc_ends[None, :-1]).astype(jnp.int32), axis=1)).astype(jnp.int32)
    owners = segment[:, None] == jnp.arange(doc_lengths.shape[0], dtype=jnp.int32)[None, :]
    doc_first = lax.optimization_barrier(jnp.sum(jnp.where(owners, doc_starts[None, :], 0), axis=1)).astype(jnp.int32)
    return (segment, places - doc_first)

def rotary_tables(position):
    frequency = jnp.exp(jnp.arange(ROT // 2, dtype=jnp.float32) * (-2.0 * math.log(10000.0) / ROT))
    angles = position.astype(jnp.float32)[:, None] * frequency[None, :]
    cosine_table = jnp.cos(angles)
    sine_table = jnp.sin(angles)
    return (jnp.concatenate([cosine_table, cosine_table], axis=1), jnp.concatenate([sine_table, sine_table], axis=1))

def rotate(values, cosine_table, sine_table):
    half_rot = ROT // 2
    rot_part = values[..., :ROT]
    turned = jnp.concatenate([-rot_part[..., half_rot:], rot_part[..., :half_rot]], axis=-1)
    rotated = rot_part * cosine_table[:, None, :] + turned * sine_table[:, None, :]
    return jnp.concatenate([rotated, values[..., ROT:]], axis=-1)

def attention(queries, keys, values, segment):
    block_rows = min(512, LEN)
    score_scale = 1.0 / math.sqrt(HEAD_DIM)
    columns = jnp.arange(LEN, dtype=jnp.int32)

    def score_block(block_number):
        block_first = (block_number * block_rows).astype(jnp.int32)
        q_block = lax.dynamic_slice_in_dim(queries, block_first, block_rows, 0)
        seg_block = lax.dynamic_slice_in_dim(segment, block_first, block_rows, 0)
        rows_here = block_first + jnp.arange(block_rows, dtype=jnp.int32)
        logits = jnp.einsum('qhe,khe->hqk', q_block, keys, precision=lax.Precision.HIGHEST) * score_scale
        logits = low_back(logits)
        allowed = (seg_block[:, None] == segment[None, :]) & (columns[None, :] <= rows_here[:, None])
        logits = jnp.where(allowed[None], logits, -1e+30)
        row_max = lax.optimization_barrier(jnp.max(logits, axis=-1, keepdims=True))
        expons = jnp.exp(logits - row_max)
        probability = low(expons / lax.optimization_barrier(jnp.sum(expons, axis=-1, keepdims=True)))
        return jnp.einsum('hqk,khe->qhe', probability, values, precision=lax.Precision.HIGHEST)
    blocks = lax.map(jax.checkpoint(score_block), jnp.arange(LEN // block_rows, dtype=jnp.int32))
    return blocks.reshape(LEN, HEADS * HEAD_DIM)

def forward(residual, params, segment, cosine_table, sine_table):
    gain_one, shift_one, w_qkv, b_qkv, w_out, gain_two, shift_two, w_gate_up, w_down = params
    normed_one = low(layer_norm(residual, gain_one, shift_one))
    projected = low_back(jnp.einsum('td,dce->tce', normed_one, w_qkv, precision=lax.Precision.HIGHEST) + b_qkv)
    queries = low(rotate(projected[:, 0].reshape(LEN, HEADS, HEAD_DIM), cosine_table, sine_table))
    keys = low(rotate(projected[:, 1].reshape(LEN, HEADS, HEAD_DIM), cosine_table, sine_table))
    values = low(projected[:, 2].reshape(LEN, HEADS, HEAD_DIM))
    attended = low_back(low(attention(queries, keys, values, segment)))
    branch = low_back(jnp.einsum('te,fe->tf', attended, w_out, precision=lax.Precision.HIGHEST))
    middle = residual + branch
    normed_two = low(layer_norm(middle, gain_two, shift_two))
    gate_up = low_back(jnp.einsum('td,dcf->tcf', normed_two, w_gate_up, precision=lax.Precision.HIGHEST))
    hidden = low(jax.nn.silu(gate_up[:, 0]) * gate_up[:, 1])
    mlp_out = low_back(jnp.einsum('tf,df->td', hidden, w_down, precision=lax.Precision.HIGHEST))
    return middle + mlp_out

def reference(tokens, lengths, ln1_gain, ln1_bias, qkv_weight, qkv_bias, out_weight, ln2_gain, ln2_bias, gate_up_weight, down_weight, cotangent):
    params = tuple((weight.astype(jnp.float32) for weight in (ln1_gain, ln1_bias, qkv_weight, qkv_bias, out_weight, ln2_gain, ln2_bias, gate_up_weight, down_weight)))

    def scan_step(totals, seq_item):
        seq_tokens, seq_grads, seq_lengths = seq_item
        segment, position = doc_tables(seq_lengths, LEN)
        cosine_table, sine_table = rotary_tables(position)

        def run_layer(residual, layer_params):
            return forward(residual, layer_params, segment, cosine_table, sine_table)
        layer_out, pull_back = jax.vjp(run_layer, seq_tokens.astype(jnp.float32), params)
        d_tokens, d_params = pull_back(seq_grads.astype(jnp.float32))
        totals = jax.tree.map(lambda left_val, right_val: left_val + right_val, totals, d_params)
        return (totals, (layer_out.astype(jnp.bfloat16), d_tokens.astype(jnp.bfloat16)))
    zero_grads = jax.tree.map(jnp.zeros_like, params)
    totals, (activations, input_grads) = lax.scan(scan_step, zero_grads, (tokens, cotangent, lengths))
    return (activations, input_grads, totals[0], totals[1], totals[2], totals[3], totals[4], totals[5], totals[6], totals[7], totals[8])
```

```python
import math

import jax
import jax.numpy as jnp
from jax import lax
from jax.experimental import pallas as pl
from jax.experimental.pallas import tpu as pltpu
from jax.sharding import PartitionSpec as P

HEAD_DIM = 64
ROT = 16
BF16 = jnp.bfloat16
F32 = jnp.float32
MIB = 1024 * 1024

SWAP_X = [(0, 1), (1, 0), (2, 3), (3, 2)]
SWAP_Y = [(0, 2), (2, 0), (1, 3), (3, 1)]
SWAP_CORE = [(0, 1), (1, 0)]


def to_x(values):
    return lax.ppermute(values, "gy", SWAP_X)


def to_y(values):
    return lax.ppermute(values, "gy", SWAP_Y)


def to_core(values):
    return lax.ppermute(values, "gz", SWAP_CORE)


def dot_nn(left, right):
    return lax.dot_general(left, right, (((1,), (0,)), ((), ())), preferred_element_type=F32)


def dot_nt(left, right):
    return lax.dot_general(left, right, (((1,), (1,)), ((), ())), preferred_element_type=F32)


def dot_tn(left, right):
    return lax.dot_general(left, right, (((0,), (0,)), ((), ())), preferred_element_type=F32)


def dot_tt(left, right):
    return lax.dot_general(left, right, (((0,), (1,)), ((), ())), preferred_element_type=F32)


VM = pl.BlockSpec(memory_space=pltpu.VMEM)
SM = pl.BlockSpec(memory_space=pltpu.SMEM)
ANY = pl.BlockSpec(memory_space=pl.ANY)


def params(limit):
    return pltpu.CompilerParams(vmem_limit_bytes=limit * MIB)


def cost(flops, moved):
    return pl.CostEstimate(flops=int(flops), bytes_accessed=int(moved), transcendentals=0)


def gather_plane(block):
    half = block.shape[0] // 2
    from_x = to_x(block)
    from_y = to_y(block)
    far_top = to_x(from_y[:half])
    far_bottom = to_y(from_x[half:])
    own = [(block, 0, 0), (from_x, 1, 0), (from_y, 2, 0), (far_top, 3, 0), (far_bottom, 3, half)]
    other = [(to_core(piece), chunk + 4, row) for piece, chunk, row in own]
    return own + other


def scatter_plane(own, sibling, rows):
    half = rows // 2
    came = to_core(sibling)

    def part(chunk, first):
        at = chunk * rows + first
        return own[at : at + half].astype(F32) + came[at : at + half].astype(F32)

    far_top = to_x(part(3, 0).astype(BF16))
    far_bottom = to_y(part(3, half).astype(BF16))
    x_top = to_x(part(1, 0).astype(BF16))
    y_bottom = to_y(part(2, half).astype(BF16))
    y_top = to_y((part(2, 0) + far_top.astype(F32)).astype(BF16))
    x_bottom = to_x((part(1, half) + far_bottom.astype(F32)).astype(BF16))
    return own, came, x_top, x_bottom, y_top, y_bottom


def summed(own_ref, came_ref, x_top, x_bottom, y_top, y_bottom):
    half = x_top.shape[0]
    total = own_ref[...].astype(F32) + came_ref[...].astype(F32)
    top = total[:half] + x_top[...].astype(F32) + y_top[...].astype(F32)
    bottom = total[half:] + x_bottom[...].astype(F32) + y_bottom[...].astype(F32)
    return jnp.concatenate([top, bottom], axis=0)


def summed_specs(rows, width):
    first = pl.BlockSpec((rows, width), lambda i: (0, 0))
    half = pl.BlockSpec((rows // 2, width), lambda i: (0, 0))
    return [first, first, half, half, half, half]


def sum_all(vectors, axes):
    for name, size in axes:
        step = 1
        while step < size:
            vectors = vectors + lax.ppermute(vectors, name, [(i, i ^ step) for i in range(size)])
            step *= 2
    return vectors


def norm_parts(values):
    average = jnp.mean(values, axis=-1, keepdims=True)
    centered = values - average
    variance = jnp.mean(centered * centered, axis=-1, keepdims=True)
    rstd = lax.rsqrt(variance + 1e-05)
    return centered * rstd, rstd


def norm_one(tokens, gain, shift):
    def body(t_ref, g_ref, b_ref, o_ref):
        xhat, _ = norm_parts(t_ref[...].astype(F32))
        o_ref[...] = (xhat * g_ref[...] + b_ref[...]).astype(BF16)

    return pl.pallas_call(
        body,
        out_shape=jax.ShapeDtypeStruct(tokens.shape, BF16),
        in_specs=[VM] * 3,
        out_specs=VM,
        compiler_params=params(24),
        cost_estimate=cost(0, 4 * tokens.size),
        name="norm_one",
    )(tokens, gain, shift)


def middle_norm(tokens, parts, gain, shift):
    rows, width = tokens.shape

    def body(t_ref, *refs):
        g_ref, b_ref, m_ref, o_ref = refs[6:]
        middle = t_ref[...].astype(F32) + summed(*refs[:6])
        m_ref[...] = middle
        xhat, _ = norm_parts(middle)
        o_ref[...] = (xhat * g_ref[...] + b_ref[...]).astype(BF16)

    whole = pl.BlockSpec((rows, width), lambda i: (0, 0))
    line = pl.BlockSpec((1, width), lambda i: (0, 0))
    return pl.pallas_call(
        body,
        grid=(1,),
        out_shape=[
            jax.ShapeDtypeStruct((rows, width), F32),
            jax.ShapeDtypeStruct((rows, width), BF16),
        ],
        in_specs=[whole] + summed_specs(rows, width) + [line, line],
        out_specs=[whole, whole],
        compiler_params=params(40),
        cost_estimate=cost(0, 14 * tokens.size),
        name="middle_norm",
    )(tokens, *parts, gain, shift)


def norm_back(values, upstream, parts, gain, out_type):
    rows, width = values.shape
    with_wide = out_type is None

    def body(v_ref, u_ref, *refs):
        g_ref = refs[6]
        outs = refs[7:]
        e = summed(*refs[:6])
        xhat, rstd = norm_parts(v_ref[...].astype(F32))
        d_xhat = e * g_ref[...]
        mean_d = jnp.mean(d_xhat, axis=-1, keepdims=True)
        mean_x = jnp.mean(d_xhat * xhat, axis=-1, keepdims=True)
        d_v = rstd * (d_xhat - mean_d - xhat * mean_x)
        total = u_ref[...].astype(F32) + d_v
        outs[0][...] = total.astype(BF16)
        outs[1][...] = jnp.concatenate(
            [jnp.sum(e * xhat, axis=0, keepdims=True), jnp.sum(e, axis=0, keepdims=True)], axis=0
        )
        if with_wide:
            outs[2][...] = total

    whole = pl.BlockSpec((rows, width), lambda i: (0, 0))
    line = pl.BlockSpec((1, width), lambda i: (0, 0))
    two = pl.BlockSpec((2, width), lambda i: (0, 0))
    return pl.pallas_call(
        body,
        grid=(1,),
        out_shape=[
            jax.ShapeDtypeStruct((rows, width), BF16),
            jax.ShapeDtypeStruct((2, width), F32),
        ]
        + ([jax.ShapeDtypeStruct((rows, width), F32)] if with_wide else []),
        in_specs=[whole, whole] + summed_specs(rows, width) + [line],
        out_specs=[whole, two] + ([whole] if with_wide else []),
        compiler_params=params(48),
        cost_estimate=cost(0, 16 * values.size),
        name="norm_back",
    )(values, upstream, *parts, gain)


def start_pieces(pos_ref, layout, piece_refs, rows, hold, sems):
    copies = []
    for number, ((chunk, first), ref) in enumerate(zip(layout, piece_refs)):
        at = pl.multiple_of(pos_ref[chunk] * rows + first, 16)
        copy = pltpu.make_async_copy(ref, hold.at[pl.ds(at, ref.shape[0]), :], sems.at[number])
        copy.start()
        copies.append((chunk, copy))
    return copies


def chunk_lanes(pos_ref, chunk, rows):
    return pl.ds(pl.multiple_of(pos_ref[chunk] * rows, rows), rows)


def project(pos, pieces, weight, bias, cosine, sine):
    layout = [(chunk, first) for _, chunk, first in pieces]
    arrays = [piece for piece, _, _ in pieces]
    rows, depth = arrays[0].shape
    length = 8 * rows
    parts, _, part_rows, width = weight.shape
    count = len(arrays)
    half_rot = ROT // 2

    def body(pos_ref, w_ref, b_ref, c_ref, s_ref, *refs):
        piece_refs = refs[:count]
        out_ref, all_ref, hold, w_hold, sems, w_sems, out_sem = refs[count:]
        w_copies = []
        for part in range(parts):
            copy = pltpu.make_async_copy(
                w_ref.at[part],
                w_hold.at[:, pl.ds(part * part_rows, part_rows), :],
                w_sems.at[part],
            )
            copy.start()
            w_copies.append(copy)
        copies = start_pieces(pos_ref, layout, piece_refs, rows, hold, sems)
        for copy in w_copies:
            copy.wait()
        for chunk in range(8):
            for owner, copy in copies:
                if owner == chunk:
                    copy.wait()
            lanes = chunk_lanes(pos_ref, chunk, rows)
            block = hold[lanes, :]
            cosines, sines = c_ref[:, lanes], s_ref[:, lanes]
            for kind in range(3):
                turned = dot_nn(block, w_hold[kind]).T + b_ref[kind * width : (kind + 1) * width, :]
                if kind < 2:
                    bands = []
                    for first in range(0, width, HEAD_DIM):
                        r_one = turned[first : first + half_rot]
                        r_two = turned[first + half_rot : first + ROT]
                        bands.append(r_one * cosines - r_two * sines)
                        bands.append(r_two * cosines + r_one * sines)
                        bands.append(turned[first + ROT : first + HEAD_DIM])
                    turned = jnp.concatenate(bands, axis=0)
                if kind == 0:
                    turned = turned * (1.0 / math.sqrt(HEAD_DIM))
                out_ref[kind * width : (kind + 1) * width, lanes] = turned.astype(BF16)
        back = pltpu.make_async_copy(hold, all_ref, out_sem)
        back.start()
        back.wait()

    return pl.pallas_call(
        body,
        out_shape=[
            jax.ShapeDtypeStruct((3 * width, length), BF16),
            jax.ShapeDtypeStruct((length, depth), BF16),
        ],
        in_specs=[SM, ANY, VM, VM, VM] + [ANY] * count,
        out_specs=[VM, ANY],
        scratch_shapes=[
            pltpu.VMEM((length, depth), BF16),
            pltpu.VMEM((3, depth, width), BF16),
            pltpu.SemaphoreType.DMA((count,)),
            pltpu.SemaphoreType.DMA((parts,)),
            pltpu.SemaphoreType.DMA,
        ],
        compiler_params=params(40),
        cost_estimate=cost(6 * length * depth * width, 20 * MIB),
        name="project",
    )(pos, weight, bias, cosine, sine, *arrays)


def hidden_back(pos, pieces, weight):
    layout = [(chunk, first) for _, chunk, first in pieces]
    arrays = [piece for piece, _, _ in pieces]
    rows, depth = arrays[0].shape
    length = 8 * rows
    parts, units, part_rows = weight.shape
    count = len(arrays)

    def body(pos_ref, w_ref, *refs):
        piece_refs = refs[:count]
        out_ref, all_ref, hold, w_hold, sems, w_sems, out_sem = refs[count:]
        w_copies = []
        for part in range(parts):
            copy = pltpu.make_async_copy(
                w_ref.at[part],
                w_hold.at[:, pl.ds(part * part_rows, part_rows)],
                w_sems.at[part],
            )
            copy.start()
            w_copies.append(copy)
        copies = start_pieces(pos_ref, layout, piece_refs, rows, hold, sems)
        for copy in w_copies:
            copy.wait()
        for chunk in range(8):
            for owner, copy in copies:
                if owner == chunk:
                    copy.wait()
            lanes = chunk_lanes(pos_ref, chunk, rows)
            out_ref[:, lanes] = dot_nt(w_hold[...], hold[lanes, :]).astype(BF16)
        back = pltpu.make_async_copy(hold, all_ref, out_sem)
        back.start()
        back.wait()

    return pl.pallas_call(
        body,
        out_shape=[
            jax.ShapeDtypeStruct((units, length), BF16),
            jax.ShapeDtypeStruct((length, depth), BF16),
        ],
        in_specs=[SM, ANY] + [ANY] * count,
        out_specs=[VM, ANY],
        scratch_shapes=[
            pltpu.VMEM((length, depth), BF16),
            pltpu.VMEM((units, depth), BF16),
            pltpu.SemaphoreType.DMA((count,)),
            pltpu.SemaphoreType.DMA((parts,)),
            pltpu.SemaphoreType.DMA,
        ],
        compiler_params=params(40),
        cost_estimate=cost(2 * length * depth * units, 23 * MIB),
        name="hidden_back",
    )(pos, weight, *arrays)


def feed(pos, pieces, weight, d_hidden):
    layout = [(chunk, first) for _, chunk, first in pieces]
    arrays = [piece for piece, _, _ in pieces]
    rows, depth = arrays[0].shape
    length = 8 * rows
    parts, pair_units, part_rows = weight.shape
    units = pair_units // 2
    count = len(arrays)

    def body(pos_ref, w_ref, dh_ref, *refs):
        piece_refs = refs[:count]
        hid_ref, dgu_ref, sib_ref, all_ref, hold, w_hold, sems, w_sems, out_sem = refs[count:]
        w_copies = []
        for part in range(parts):
            copy = pltpu.make_async_copy(
                w_ref.at[part],
                w_hold.at[:, pl.ds(part * part_rows, part_rows)],
                w_sems.at[part],
            )
            copy.start()
            w_copies.append(copy)
        copies = start_pieces(pos_ref, layout, piece_refs, rows, hold, sems)
        for copy in w_copies:
            copy.wait()
        for chunk in range(8):
            for owner, copy in copies:
                if owner == chunk:
                    copy.wait()
            lanes = chunk_lanes(pos_ref, chunk, rows)
            block = hold[lanes, :]
            gate = dot_nt(w_hold[:units, :], block)
            up = dot_nt(w_hold[units:, :], block)
            d_hid = dh_ref[:, lanes].astype(F32)
            sig = 1.0 / (1.0 + jnp.exp(-gate))
            silu = gate * sig
            hid_ref[:, lanes] = (silu * up).astype(BF16)
            dgu_ref[:units, lanes] = (d_hid * up * sig * (1.0 + gate * (1.0 - sig))).astype(BF16)
            dgu_ref[units:, lanes] = (d_hid * silu).astype(BF16)
        back = pltpu.make_async_copy(hold, all_ref, out_sem)
        back.start()
        for chunk in range(4):
            lanes = chunk_lanes(pos_ref, chunk + 4, rows)
            sib_ref[chunk * rows : (chunk + 1) * rows, :] = dot_tn(
                dgu_ref[:, lanes], w_hold[...]
            ).astype(BF16)
        back.wait()

    return pl.pallas_call(
        body,
        out_shape=[
            jax.ShapeDtypeStruct((units, length), BF16),
            jax.ShapeDtypeStruct((pair_units, length), BF16),
            jax.ShapeDtypeStruct((4 * rows, depth), BF16),
            jax.ShapeDtypeStruct((length, depth), BF16),
        ],
        in_specs=[SM, ANY, VM] + [ANY] * count,
        out_specs=[VM, VM, VM, ANY],
        scratch_shapes=[
            pltpu.VMEM((length, depth), BF16),
            pltpu.VMEM((pair_units, depth), BF16),
            pltpu.SemaphoreType.DMA((count,)),
            pltpu.SemaphoreType.DMA((parts,)),
            pltpu.SemaphoreType.DMA,
        ],
        compiler_params=params(56),
        cost_estimate=cost(3 * length * depth * pair_units, 40 * MIB),
        name="feed",
    )(pos, weight, d_hidden, *arrays)


def rows_half(pos, left, weight, first, dot_kind, name):
    length = left.shape[1]
    rows = length // 8
    if dot_kind == "tn":
        parts, depth, part_cols = weight.shape
        width = parts * part_cols
    else:
        width, depth = weight.shape

    def body(pos_ref, l_ref, w_ref, o_ref):
        block = l_ref[...]
        if dot_kind == "tn":
            for part in range(parts):
                o_ref[:, part * part_cols : (part + 1) * part_cols] = dot_tn(
                    block, w_ref[part]
                ).astype(BF16)
        else:
            o_ref[...] = dot_tt(block, w_ref[...]).astype(BF16)

    rank = len(weight.shape)
    return pl.pallas_call(
        body,
        grid_spec=pltpu.PrefetchScalarGridSpec(
            num_scalar_prefetch=1,
            grid=(4,),
            in_specs=[
                pl.BlockSpec((left.shape[0], rows), lambda i, p: (0, p[first + i])),
                pl.BlockSpec(weight.shape, lambda i, p: (0,) * rank, pipeline_mode=pl.Buffered(1)),
            ],
            out_specs=pl.BlockSpec((rows, width), lambda i, p: (i, 0)),
        ),
        out_shape=jax.ShapeDtypeStruct((4 * rows, width), BF16),
        compiler_params=params(32),
        cost_estimate=cost(length * left.shape[0] * width, 12 * MIB),
        name=name,
    )(pos, left, weight)


def rows_half_qkv(pos, left, weight, first):
    length = left.shape[1]
    rows = length // 8
    parts, _, part_cols, width = weight.shape
    depth = parts * part_cols

    def body(pos_ref, l_ref, w_ref, o_ref):
        for part in range(parts):
            total = dot_tt(l_ref[:width], w_ref[part, 0])
            total += dot_tt(l_ref[width : 2 * width], w_ref[part, 1])
            total += dot_tt(l_ref[2 * width :], w_ref[part, 2])
            o_ref[:, part * part_cols : (part + 1) * part_cols] = total.astype(BF16)

    return pl.pallas_call(
        body,
        grid_spec=pltpu.PrefetchScalarGridSpec(
            num_scalar_prefetch=1,
            grid=(4,),
            in_specs=[
                pl.BlockSpec((3 * width, rows), lambda i, p: (0, p[first + i])),
                pl.BlockSpec(weight.shape, lambda i, p: (0, 0, 0, 0), pipeline_mode=pl.Buffered(1)),
            ],
            out_specs=pl.BlockSpec((rows, depth), lambda i, p: (i, 0)),
        ),
        out_shape=jax.ShapeDtypeStruct((4 * rows, depth), BF16),
        compiler_params=params(32),
        cost_estimate=cost(3 * length * width * depth, 10 * MIB),
        name="qkv_rows",
    )(pos, left, weight)


def weight_grad(left, right, parts, name):
    height, length = left.shape
    part_cols = right.shape[1] // parts

    def body(l_ref, r_ref, o_ref):
        o_ref[0] = dot_nn(l_ref[...], r_ref[...]).astype(BF16)

    return pl.pallas_call(
        body,
        grid=(parts,),
        in_specs=[
            pl.BlockSpec((height, length), lambda i: (0, 0), pipeline_mode=pl.Buffered(1)),
            pl.BlockSpec((length, part_cols), lambda i: (0, i)),
        ],
        out_specs=pl.BlockSpec((1, height, part_cols), lambda i: (i, 0, 0)),
        out_shape=jax.ShapeDtypeStruct((parts, height, part_cols), BF16),
        compiler_params=params(40),
        cost_estimate=cost(2 * height * length * right.shape[1], 20 * MIB),
        name=name,
    )(left, right)


def attention_grads(d_projected, tokens, attended, d_branch, parts):
    width, length = attended.shape
    part_rows = tokens.shape[1] // parts

    def body(dp_ref, x_ref, a_ref, db_ref, o_ref):
        for kind in range(3):
            grad = dot_nn(dp_ref[kind * width : (kind + 1) * width, :], x_ref[...])
            o_ref[0, kind] = grad.T.astype(BF16)
        o_ref[0, 3] = dot_nn(a_ref[...], db_ref[...]).T.astype(BF16)

    return pl.pallas_call(
        body,
        grid=(parts,),
        in_specs=[
            pl.BlockSpec((3 * width, length), lambda i: (0, 0), pipeline_mode=pl.Buffered(1)),
            pl.BlockSpec((length, part_rows), lambda i: (0, i)),
            pl.BlockSpec((width, length), lambda i: (0, 0), pipeline_mode=pl.Buffered(1)),
            pl.BlockSpec((length, part_rows), lambda i: (0, i)),
        ],
        out_specs=pl.BlockSpec((1, 4, part_rows, width), lambda i: (i, 0, 0, 0)),
        out_shape=jax.ShapeDtypeStruct((parts, 4, part_rows, width), BF16),
        compiler_params=params(40),
        cost_estimate=cost(8 * width * length * tokens.shape[1], 24 * MIB),
        name="attention_grads",
    )(d_projected, tokens, attended, d_branch)


def allowed_pairs(first_ref, q_at, k_at, size):
    lanes = pl.ds(pl.multiple_of(q_at * size, size), size)
    k_index = k_at * size + lax.broadcasted_iota(jnp.int32, (size, size), 0)
    q_index = q_at * size + lax.broadcasted_iota(jnp.int32, (size, size), 1)
    return (k_index >= first_ref[:, lanes]) & (k_index <= q_index)


def attend(qkv, doc_first, start_block, size):
    length = qkv.shape[1]
    width = qkv.shape[0] // 3
    heads = width // HEAD_DIM

    def body(start_ref, qkv_ref, first_ref, out_ref, log_ref):
        def query_block(q_at, _):
            q_lanes = pl.ds(pl.multiple_of(q_at * size, size), size)

            def key_block(k_at, carry):
                k_lanes = pl.ds(pl.multiple_of(k_at * size, size), size)
                mask = allowed_pairs(first_ref, q_at, k_at, size)
                new = []
                for head in range(heads):
                    top, total, acc = carry[head]
                    at = head * HEAD_DIM
                    query = qkv_ref[at : at + HEAD_DIM, q_lanes]
                    key = qkv_ref[width + at : width + at + HEAD_DIM, k_lanes]
                    value = qkv_ref[2 * width + at : 2 * width + at + HEAD_DIM, k_lanes]
                    logits = jnp.where(mask, dot_tn(key, query), -1e30)
                    new_top = jnp.maximum(top, jnp.max(logits, axis=0, keepdims=True))
                    shrink = jnp.exp(top - new_top)
                    expons = jnp.exp(logits - new_top)
                    total = total * shrink + jnp.sum(expons, axis=0, keepdims=True)
                    acc = acc * shrink + dot_nn(value, expons.astype(BF16))
                    new.append((new_top, total, acc))
                return tuple(new)

            zero = tuple(
                (
                    jnp.full((1, size), -1e30, F32),
                    jnp.zeros((1, size), F32),
                    jnp.zeros((HEAD_DIM, size), F32),
                )
                for _ in range(heads)
            )
            done = lax.fori_loop(start_ref[q_at], q_at + 1, key_block, zero)
            for head in range(heads):
                top, total, acc = done[head]
                at = head * HEAD_DIM
                out_ref[at : at + HEAD_DIM, q_lanes] = (acc / total).astype(BF16)
                log_ref[head : head + 1, q_lanes] = top + jnp.log(total)
            return 0

        lax.fori_loop(0, length // size, query_block, 0)

    return pl.pallas_call(
        body,
        out_shape=[
            jax.ShapeDtypeStruct((width, length), BF16),
            jax.ShapeDtypeStruct((heads, length), F32),
        ],
        in_specs=[SM, VM, VM],
        out_specs=[VM, VM],
        compiler_params=params(32),
        cost_estimate=cost(12e9, 5 * MIB),
        name="attend",
    )(start_block, qkv, doc_first)


def attend_back(
    pos, pieces, out_weight, qkv, attended, log_sums, cosine, sine, doc_first, start_block, size
):
    layout = [(chunk, first) for _, chunk, first in pieces]
    arrays = [piece for piece, _, _ in pieces]
    rows, depth = arrays[0].shape
    length = 8 * rows
    width = attended.shape[0]
    heads = width // HEAD_DIM
    count = len(arrays)
    half_rot = ROT // 2
    scale = 1.0 / math.sqrt(HEAD_DIM)

    def body(pos_ref, start_ref, w_ref, qkv_ref, att_ref, log_ref, c_ref, s_ref, first_ref, *refs):
        piece_refs = refs[:count]
        out_ref, bias_ref, all_ref, hold, d_att, grads, sems, out_sem = refs[count:]
        copies = start_pieces(pos_ref, layout, piece_refs, rows, hold, sems)
        grads[...] = jnp.zeros_like(grads)
        for chunk in range(8):
            for owner, copy in copies:
                if owner == chunk:
                    copy.wait()
            lanes = chunk_lanes(pos_ref, chunk, rows)
            d_att[:, lanes] = dot_tt(w_ref[...], hold[lanes, :]).astype(BF16)
        back = pltpu.make_async_copy(hold, all_ref, out_sem)
        back.start()

        def query_block(q_at, _):
            q_lanes = pl.ds(pl.multiple_of(q_at * size, size), size)
            deltas = []
            for head in range(heads):
                at = head * HEAD_DIM
                deltas.append(
                    jnp.sum(
                        d_att[at : at + HEAD_DIM, q_lanes].astype(F32)
                        * att_ref[at : at + HEAD_DIM, q_lanes].astype(F32),
                        axis=0,
                        keepdims=True,
                    )
                )

            def key_block(k_at, _):
                k_lanes = pl.ds(pl.multiple_of(k_at * size, size), size)
                mask = allowed_pairs(first_ref, q_at, k_at, size)
                for head in range(heads):
                    at = head * HEAD_DIM
                    key_at, value_at = width + at, 2 * width + at
                    query = qkv_ref[at : at + HEAD_DIM, q_lanes]
                    key = qkv_ref[key_at : key_at + HEAD_DIM, k_lanes]
                    value = qkv_ref[value_at : value_at + HEAD_DIM, k_lanes]
                    d_out = d_att[at : at + HEAD_DIM, q_lanes]
                    logits = dot_tn(key, query)
                    prob = jnp.where(
                        mask, jnp.exp(logits - log_ref[head : head + 1, q_lanes]), 0.0
                    )
                    d_prob = dot_tn(value, d_out)
                    d_logits = (prob * (d_prob - deltas[head])).astype(BF16)
                    grads[at : at + HEAD_DIM, q_lanes] += dot_nn(key, d_logits)
                    grads[key_at : key_at + HEAD_DIM, k_lanes] += dot_nt(query, d_logits)
                    grads[value_at : value_at + HEAD_DIM, k_lanes] += dot_nt(
                        d_out, prob.astype(BF16)
                    )
                return 0

            lax.fori_loop(start_ref[q_at], q_at + 1, key_block, 0)
            return 0

        lax.fori_loop(0, length // size, query_block, 0)

        bias_ref[...] = jnp.zeros_like(bias_ref)

        def finish(at, _):
            lanes = pl.ds(pl.multiple_of(at * rows, rows), rows)
            cosines, sines = c_ref[:, lanes], s_ref[:, lanes]
            for kind in range(3):
                band = grads[kind * width : (kind + 1) * width, lanes]
                if kind == 0:
                    band = band * scale
                if kind < 2:
                    bands = []
                    for first in range(0, width, HEAD_DIM):
                        g_one = band[first : first + half_rot]
                        g_two = band[first + half_rot : first + ROT]
                        bands.append(g_one * cosines + g_two * sines)
                        bands.append(g_two * cosines - g_one * sines)
                        bands.append(band[first + ROT : first + HEAD_DIM])
                    band = jnp.concatenate(bands, axis=0)
                low = band.astype(BF16)
                out_ref[kind * width : (kind + 1) * width, lanes] = low
                bias_ref[kind * width : (kind + 1) * width, :] += jnp.sum(
                    low.astype(F32), axis=1, keepdims=True
                )
            return 0

        lax.fori_loop(0, length // rows, finish, 0)
        back.wait()

    return pl.pallas_call(
        body,
        out_shape=[
            jax.ShapeDtypeStruct((3 * width, length), BF16),
            jax.ShapeDtypeStruct((3 * width, 1), F32),
            jax.ShapeDtypeStruct((length, depth), BF16),
        ],
        in_specs=[SM, SM] + [VM] * 7 + [ANY] * count,
        out_specs=[VM, VM, ANY],
        scratch_shapes=[
            pltpu.VMEM((length, depth), BF16),
            pltpu.VMEM((width, length), BF16),
            pltpu.VMEM((3 * width, length), F32),
            pltpu.SemaphoreType.DMA((count,)),
            pltpu.SemaphoreType.DMA,
        ],
        compiler_params=params(48),
        cost_estimate=cost(35e9, 28 * MIB),
        name="attend_back",
    )(
        pos,
        start_block,
        out_weight,
        qkv,
        attended,
        log_sums,
        cosine,
        sine,
        doc_first,
        *arrays,
    )


def doc_tables(doc_lengths, seq_length):
    doc_ends = jnp.cumsum(doc_lengths)
    doc_starts = doc_ends - doc_lengths
    places = jnp.arange(seq_length, dtype=jnp.int32)
    segment = jnp.sum((places[:, None] >= doc_ends[None, :-1]).astype(jnp.int32), axis=1)
    owners = segment[:, None] == jnp.arange(doc_lengths.shape[0], dtype=jnp.int32)[None, :]
    return places, jnp.sum(jnp.where(owners, doc_starts[None, :], 0), axis=1)


def shards(
    tokens,
    lengths,
    ln1_gain,
    ln1_bias,
    qkv_weight,
    qkv_bias,
    out_weight,
    ln2_gain,
    ln2_bias,
    gate_up_weight,
    down_weight,
    cotangent,
    axes,
):
    x = tokens[0]
    cot = cotangent[0]
    rows, depth = x.shape
    length = 8 * rows
    parts = axes["gx"]
    part_rows = depth // parts
    width = qkv_weight.shape[2]
    units = gate_up_weight.shape[2]
    size = 256
    gain_one = ln1_gain.astype(F32)[None]
    shift_one = ln1_bias.astype(F32)[None]
    gain_two = ln2_gain.astype(F32)[None]
    shift_two = ln2_bias.astype(F32)[None]

    w_qkv = lax.all_gather(qkv_weight.transpose(1, 0, 2), "gx", axis=0, tiled=False)
    w_out = lax.all_gather(out_weight, "gx", axis=0, tiled=False).reshape(depth, width)
    w_down = lax.all_gather(down_weight.T, "gx", axis=0, tiled=False)
    w_gate_up = lax.all_gather(
        gate_up_weight.transpose(1, 2, 0).reshape(2 * units, part_rows), "gx", axis=0, tiled=False
    )

    steps = jnp.arange(8, dtype=jnp.int32)
    pos = (lax.axis_index("gy") ^ (steps % 4)) * 2 + (lax.axis_index("gz") ^ (steps // 4))
    places, doc_first = doc_tables(lengths[0], length)
    start_block = doc_first[:: size] // size
    frequency = jnp.exp(
        jnp.arange(ROT // 2, dtype=F32) * (-2.0 * math.log(10000.0) / ROT)
    )
    angles = frequency[:, None] * (places - doc_first).astype(F32)[None, :]
    cosine, sine = jnp.cos(angles), jnp.sin(angles)
    doc_first = doc_first[None]

    normed_one = norm_one(x, gain_one, shift_one)
    qkv, all_one = project(
        pos,
        gather_plane(normed_one),
        w_qkv,
        qkv_bias.astype(F32).reshape(3 * width, 1),
        cosine,
        sine,
    )
    attended, log_sums = attend(qkv, doc_first, start_block, size)
    out_sib = rows_half(pos, attended, w_out, 4, "tt", "out_rows_sibling")
    out_own = rows_half(pos, attended, w_out, 0, "tt", "out_rows_own")
    middle, normed_two = middle_norm(
        x, scatter_plane(out_own, out_sib, rows), gain_two, shift_two
    )

    d_hidden, all_cot = hidden_back(pos, gather_plane(cot), w_down)
    hidden, d_gate_up, d_two_sib, all_two = feed(pos, gather_plane(normed_two), w_gate_up, d_hidden)
    d_two_own = rows_half(pos, d_gate_up, w_gate_up, 0, "tn", "d_two_rows_own")
    d_two = scatter_plane(d_two_own, d_two_sib, rows)
    down_grad = weight_grad(hidden, all_cot, parts, "down_grad")
    gate_up_grad = weight_grad(d_gate_up, all_two, parts, "gate_up_grad")
    down_grad = lax.psum_scatter(down_grad, "gx", scatter_dimension=0, tiled=False)
    gate_up_grad = lax.psum_scatter(gate_up_grad, "gx", scatter_dimension=0, tiled=False)
    mlp_sib = rows_half(pos, hidden, w_down, 4, "tn", "mlp_rows_sibling")
    mlp_own = rows_half(pos, hidden, w_down, 0, "tn", "mlp_rows_own")
    mlp = scatter_plane(mlp_own, mlp_sib, rows)
    total = mlp[0][:rows].astype(F32) + mlp[1][:rows].astype(F32)
    total = total + jnp.concatenate(
        [
            mlp[2].astype(F32) + mlp[4].astype(F32),
            mlp[3].astype(F32) + mlp[5].astype(F32),
        ],
        axis=0,
    )
    activations = (middle + total).astype(BF16)

    d_branch, norm_two_sums, d_middle = norm_back(middle, cot, d_two, gain_two, None)
    d_projected, bias_sums, all_branch = attend_back(
        pos,
        gather_plane(d_branch),
        w_out,
        qkv,
        attended,
        log_sums,
        cosine,
        sine,
        doc_first,
        start_block,
        size,
    )
    d_one_sib = rows_half_qkv(pos, d_projected, w_qkv, 4)
    d_one_own = rows_half_qkv(pos, d_projected, w_qkv, 0)
    d_one = scatter_plane(d_one_own, d_one_sib, rows)
    attn_grads = attention_grads(d_projected, all_one, attended, all_branch, parts)
    attn_grads = lax.psum_scatter(attn_grads, "gx", scatter_dimension=0, tiled=False)
    input_grad, norm_one_sums = norm_back(x, d_middle, d_one, gain_one, BF16)

    norm_two_sums = sum_all(
        norm_two_sums, [("gz", axes["gz"]), ("gy", axes["gy"]), ("gx", axes["gx"])]
    )
    norm_one_sums = sum_all(
        norm_one_sums, [("gz", axes["gz"]), ("gy", axes["gy"]), ("gx", axes["gx"])]
    )
    bias_sum = sum_all(bias_sums.reshape(3, width), [("gx", axes["gx"])])
    attn_grads = attn_grads.astype(F32)
    return (
        activations[None],
        input_grad[None],
        norm_one_sums[0],
        norm_one_sums[1],
        attn_grads[:3].transpose(1, 0, 2),
        bias_sum,
        attn_grads[3],
        norm_two_sums[0],
        norm_two_sums[1],
        gate_up_grad.astype(F32).reshape(2, units, part_rows).transpose(2, 0, 1),
        down_grad.astype(F32).T,
    )


def solution(mesh):
    axes = dict(mesh.shape)
    placed = (
        P("gx", ("gy", "gz"), None),
        P("gx", None),
        P(),
        P(),
        P("gx", None, ("gy", "gz")),
        P(None, ("gy", "gz")),
        P("gx", ("gy", "gz")),
        P(),
        P(),
        P("gx", None, ("gy", "gz")),
        P("gx", ("gy", "gz")),
        P("gx", ("gy", "gz"), None),
    )
    return jax.shard_map(
        lambda *args: shards(*args, axes),
        mesh=mesh,
        in_specs=placed,
        out_specs=(
            P("gx", ("gy", "gz"), None),
            P("gx", ("gy", "gz"), None),
            P(),
            P(),
            P("gx", None, ("gy", "gz")),
            P(None, ("gy", "gz")),
            P("gx", ("gy", "gz")),
            P(),
            P(),
            P("gx", None, ("gy", "gz")),
            P("gx", ("gy", "gz")),
        ),
        check_vma=False,
    )
```

```python
import math

import jax
import jax.numpy as jnp
from jax import lax
from jax.experimental import pallas as pl
from jax.experimental.pallas import tpu as pltpu
from jax.sharding import PartitionSpec as P

HEAD_DIM = 64
ROT = 16
BF16 = jnp.bfloat16
F32 = jnp.float32
MIB = 1024 * 1024
SCALE = 1.0

SWAP_X = [(0, 1), (1, 0), (2, 3), (3, 2)]
SWAP_Y = [(0, 2), (2, 0), (1, 3), (3, 1)]
SWAP_FAR = [(0, 3), (3, 0), (1, 2), (2, 1)]
SWAP_CORE = [(0, 1), (1, 0)]


def to_x(values):
    return lax.ppermute(values, "gy", SWAP_X)


def to_y(values):
    return lax.ppermute(values, "gy", SWAP_Y)


def to_far(values):
    return lax.ppermute(values, "gy", SWAP_FAR)


def after(values, *others):
    return lax.optimization_barrier((values, others))[0]


def to_core(values):
    return lax.ppermute(values, "gz", SWAP_CORE)


def dot_nn(left, right):
    return lax.dot_general(left, right, (((1,), (0,)), ((), ())), preferred_element_type=F32)


def dot_nt(left, right):
    return lax.dot_general(left, right, (((1,), (1,)), ((), ())), preferred_element_type=F32)


def dot_tn(left, right):
    return lax.dot_general(left, right, (((0,), (0,)), ((), ())), preferred_element_type=F32)


def dot_tt(left, right):
    return lax.dot_general(left, right, (((0,), (1,)), ((), ())), preferred_element_type=F32)


VM = pl.BlockSpec(memory_space=pltpu.VMEM)
SM = pl.BlockSpec(memory_space=pltpu.SMEM)
ANY = pl.BlockSpec(memory_space=pl.ANY)


def params():
    return pltpu.CompilerParams(vmem_limit_bytes=58 * MIB)


def cost(flops, moved, scale=1):
    return pl.CostEstimate(
        flops=int(flops * scale * SCALE), bytes_accessed=int(moved * scale * SCALE), transcendentals=0
    )


def gather_first(block):
    return block, to_x(block), to_y(block), to_core(block)


def gather_plane(block, *between):
    return gather_second(gather_first(block), between)


def gather_second(first, between, later=None):
    block, from_x, from_y, other = first
    half = block.shape[0] // 2
    far_top = to_x(after(from_y[:half], *between))
    far_bottom = to_y(after(from_x[half:], *between))
    own = [(block, 0, 0), (from_x, 1, 0), (from_y, 2, 0), (far_top, 3, 0), (far_bottom, 3, half)]
    if later is not None:
        held = later(far_top, far_bottom)
        from_x, from_y, far_top, far_bottom = after((from_x, from_y, far_top, far_bottom), *held)
    return own + [
        (other, 4, 0),
        (to_core(from_x), 5, 0),
        (to_core(from_y), 6, 0),
        (to_core(far_top), 7, 0),
        (to_core(far_bottom), 7, half),
    ]


def exchange_first(own, sibling):
    came = to_core(sibling)
    sent = tuple(jnp.stack([own[step], came[step]]) for step in range(1, 4))
    return own[0], came[0], lax.optimization_barrier(sent)


def exchange_second(own, came, sent):
    return [own, came, to_x(sent[0]), to_y(sent[1]), to_far(sent[2])]


def exchanged_copies(refs, hold_of, sems):
    copies = [
        pltpu.make_async_copy(refs[0], hold_of(0), sems.at[0]),
        pltpu.make_async_copy(refs[1], hold_of(4), sems.at[4]),
    ]
    for step in range(1, 4):
        for core in range(2):
            chunk = step + 4 * core
            copies.append(
                pltpu.make_async_copy(refs[step + 1].at[core], hold_of(chunk), sems.at[chunk])
            )
    return copies


def scatter_first(own, sibling, rows):
    half = rows // 2
    came = to_core(sibling)

    def part(chunk, first):
        at = chunk * rows + first
        return (own[at : at + half].astype(F32) + came[at : at + half].astype(F32)).astype(BF16)

    for_x = jnp.concatenate([part(3, 0), part(1, 0)], axis=0)
    for_y = jnp.concatenate([part(3, half), part(2, half)], axis=0)
    return came, lax.optimization_barrier((for_x, for_y))


def scatter_second(own, came, sent, rows, *between):
    half = rows // 2
    from_x, from_y = after((to_x(sent[0]), to_y(sent[1])), *between)

    def part(chunk, first, more):
        at = chunk * rows + first
        total = own[at : at + half].astype(F32) + came[at : at + half].astype(F32)
        return (total + more.astype(F32)).astype(BF16)

    return [part(2, 0, from_x[:half]), part(1, half, from_y[:half])], [from_x, from_y]


def scatter_last(own, came, sent, arrived):
    y_top, x_bottom = to_y(sent[0]), to_x(sent[1])
    return own, came, arrived[0], x_bottom, y_top, arrived[1]


def summed(own_ref, came_ref, from_x, x_bottom, y_top, from_y):
    half = x_bottom.shape[0]
    total = own_ref[...].astype(F32) + came_ref[...].astype(F32)
    top = total[:half] + from_x[...].astype(F32) + y_top[...].astype(F32)
    bottom = total[half:] + x_bottom[...].astype(F32) + from_y[...].astype(F32)
    return jnp.concatenate([top, bottom], axis=0)


def sum_all(vectors, axes):
    for name, size in axes:
        step = 1
        while step < size:
            width = min(4, size // step)
            shifted = [
                lax.ppermute(vectors, name, [(i, i ^ (step * k)) for i in range(size)])
                for k in range(1, width)
            ]
            for other in shifted:
                vectors = vectors + other
            step *= width
    return vectors


def norm_parts(values):
    average = jnp.mean(values, axis=-1, keepdims=True)
    centered = values - average
    variance = jnp.mean(centered * centered, axis=-1, keepdims=True)
    rstd = lax.rsqrt(variance + 1e-05)
    return centered * rstd, rstd


def norm_one(tokens, gain, shift):
    def body(t_ref, g_ref, b_ref, o_ref):
        xhat, _ = norm_parts(t_ref[...].astype(F32))
        o_ref[...] = (xhat * g_ref[...] + b_ref[...]).astype(BF16)

    return pl.pallas_call(
        body,
        out_shape=jax.ShapeDtypeStruct(tokens.shape, BF16),
        in_specs=[VM] * 3,
        out_specs=VM,
        compiler_params=params(),
        cost_estimate=cost(0, 4 * tokens.size),
        name="norm_one",
    )(tokens, gain, shift)


def middle_norm(tokens, blocks, weight_pieces, gain, shift):
    rows, depth = tokens.shape
    layout, arrays = split_pieces(weight_pieces)
    width = blocks[0].shape[0]
    count = len(arrays)

    def body(t_ref, g_ref, b_ref, *refs):
        piece_refs = refs[:count]
        block_refs = refs[count : count + 5]
        m_ref, o_ref, hold, att, sems, b_sems = refs[count + 5 :]
        copies = exchanged_copies(
            block_refs, lambda chunk: att.at[pl.ds(chunk * width, width), :], b_sems
        )
        for copy in copies:
            copy.start()
        copies += [copy for _, copy in start_pieces(layout, piece_refs, width, hold, sems)]
        for copy in copies:
            copy.wait()
        middle = t_ref[...].astype(F32) + dot_tn(att[...], hold[...])
        m_ref[...] = middle
        xhat, _ = norm_parts(middle)
        o_ref[...] = (xhat * g_ref[...] + b_ref[...]).astype(BF16)

    return pl.pallas_call(
        body,
        out_shape=[
            jax.ShapeDtypeStruct((rows, depth), F32),
            jax.ShapeDtypeStruct((rows, depth), BF16),
        ],
        in_specs=[VM, VM, VM] + [ANY] * (count + 5),
        out_specs=[VM, VM],
        scratch_shapes=[
            pltpu.VMEM((8 * width, depth), BF16),
            pltpu.VMEM((8 * width, rows), BF16),
            pltpu.SemaphoreType.DMA((count,)),
            pltpu.SemaphoreType.DMA((8,)),
        ],
        compiler_params=params(),
        cost_estimate=cost(2 * rows * depth * 8 * width, 14 * MIB),
        name="middle_norm",
    )(tokens, gain, shift, *arrays, *blocks)


def norm_back_parts(v_ref, u_ref, part_refs, g_ref):
    e = summed(*part_refs)
    xhat, rstd = norm_parts(v_ref[...].astype(F32))
    d_xhat = e * g_ref[...]
    mean_d = jnp.mean(d_xhat, axis=-1, keepdims=True)
    mean_x = jnp.mean(d_xhat * xhat, axis=-1, keepdims=True)
    d_v = rstd * (d_xhat - mean_d - xhat * mean_x)
    sums = jnp.concatenate(
        [jnp.sum(e * xhat, axis=0, keepdims=True), jnp.sum(e, axis=0, keepdims=True)], axis=0
    )
    return u_ref[...].astype(F32) + d_v, sums


def norm_two_back(middle, cotangent, parts, gain, weight_pieces):
    rows, depth = middle.shape
    layout, arrays = split_pieces(weight_pieces)
    width = arrays[0].shape[0]
    count = len(arrays)

    def body(v_ref, u_ref, *refs):
        g_ref = refs[6]
        piece_refs = refs[7 : 7 + count]
        low_ref, sum_ref, wide_ref, *out_refs, hold, sems = refs[7 + count :]
        copies = start_pieces(layout, piece_refs, width, hold, sems)
        total, sum_ref[...] = norm_back_parts(v_ref, u_ref, refs[:6], g_ref)
        wide_ref[...] = total
        low_ref[...] = total.astype(BF16)
        for _, copy in copies:
            copy.wait()
        for chunk in range(8):
            block = dot_nt(hold[chunk * width : (chunk + 1) * width, :], low_ref[...]).astype(BF16)
            if chunk < 4:
                out_refs[chunk][...] = block
            else:
                out_refs[4][chunk - 4] = block

    whole = pl.BlockSpec((rows, depth), lambda i: (0, 0))
    line = pl.BlockSpec((1, depth), lambda i: (0, 0))
    two = pl.BlockSpec((2, depth), lambda i: (0, 0))
    half = pl.BlockSpec((rows // 2, depth), lambda i: (0, 0))
    second = pl.BlockSpec((rows // 2, depth), lambda i: (1, 0))
    block = pl.BlockSpec((width, rows), lambda i: (0, 0))
    outs = pl.pallas_call(
        body,
        grid=(1,),
        in_specs=[whole, whole, whole, whole, second, half, half, second, line] + [ANY] * count,
        out_specs=[whole, two, whole]
        + [block] * 4
        + [pl.BlockSpec((4, width, rows), lambda i: (0, 0, 0))],
        scratch_shapes=[
            pltpu.VMEM((8 * width, depth), BF16),
            pltpu.SemaphoreType.DMA((count,)),
        ],
        out_shape=[
            jax.ShapeDtypeStruct((rows, depth), BF16),
            jax.ShapeDtypeStruct((2, depth), F32),
            jax.ShapeDtypeStruct((rows, depth), F32),
        ]
        + [jax.ShapeDtypeStruct((width, rows), BF16)] * 4
        + [jax.ShapeDtypeStruct((4, width, rows), BF16)],
        compiler_params=params(),
        cost_estimate=cost(0, 0),
        name="norm_two_back",
    )(middle, cotangent, *parts, gain, *arrays)
    return outs[0], outs[1], outs[2], outs[3:7], outs[7]


def norm_one_back(tokens, d_middle, parts, gain):
    rows, depth = tokens.shape

    def body(v_ref, u_ref, *refs):
        g_ref, low_ref, sum_ref = refs[6:]
        total, sum_ref[...] = norm_back_parts(v_ref, u_ref, refs[:6], g_ref)
        low_ref[...] = total.astype(BF16)

    whole = pl.BlockSpec((rows, depth), lambda i: (0, 0))
    line = pl.BlockSpec((1, depth), lambda i: (0, 0))
    two = pl.BlockSpec((2, depth), lambda i: (0, 0))
    half = pl.BlockSpec((rows // 2, depth), lambda i: (0, 0))
    second = pl.BlockSpec((rows // 2, depth), lambda i: (1, 0))
    return pl.pallas_call(
        body,
        grid=(1,),
        out_shape=[
            jax.ShapeDtypeStruct((rows, depth), BF16),
            jax.ShapeDtypeStruct((2, depth), F32),
        ],
        in_specs=[whole, whole, whole, whole, second, half, half, second, line],
        out_specs=[whole, two],
        compiler_params=params(),
        cost_estimate=cost(0, 8 * MIB),
        name="norm_one_back",
    )(tokens, d_middle, *parts, gain)


def split_pieces(pieces):
    return [(chunk, first) for _, chunk, first in pieces], [piece for piece, _, _ in pieces]


def start_pieces(layout, piece_refs, rows, hold, sems, pos_ref=None):
    copies = []
    for number, ((chunk, first), ref) in enumerate(zip(layout, piece_refs)):
        if pos_ref is None:
            at = chunk * rows + first
        else:
            at = pl.multiple_of(pos_ref[chunk] * rows + first, 16)
        copy = pltpu.make_async_copy(ref, hold.at[pl.ds(at, ref.shape[0]), :], sems.at[number])
        copy.start()
        copies.append((chunk, copy))
    return copies


def column_copies(part, cols, layout, piece_refs, rows, hold, sems, pos_ref=None):
    columns = pl.ds(part * cols, cols)
    copies = []
    for number, ((chunk, first), ref) in enumerate(zip(layout, piece_refs)):
        if pos_ref is None:
            at = chunk * rows + first
        else:
            at = pl.multiple_of(pos_ref[chunk] * rows + first, 16)
        copies.append(
            pltpu.make_async_copy(
                ref.at[:, columns],
                hold.at[pl.ds(at, ref.shape[0]), columns],
                sems.at[part, number],
            )
        )
    return copies


def copy_columns(step, parts, cols, layout, piece_refs, rows, hold, sems, pos_ref=None):
    def copies(part):
        return column_copies(part, cols, layout, piece_refs, rows, hold, sems, pos_ref)

    @pl.when(step == 0)
    def _():
        for part in range(parts):
            for copy in copies(part):
                copy.start()

    for part in range(parts):

        @pl.when(step == part)
        def _(part=part):
            for copy in copies(part):
                copy.wait()


def weight_copies(w_ref, height, w_hold, w_sems):
    parts, _, cols = w_ref.shape
    return [
        pltpu.make_async_copy(
            w_ref.at[part, pl.ds(0, height)],
            w_hold.at[:, pl.ds(part * cols, cols)],
            w_sems.at[part],
        )
        for part in range(parts)
    ]


def wait_core(core_step, copies):
    for chunk, copy in copies:
        if chunk // 4 == core_step:
            copy.wait()


def project(pos, pieces, weight, bias, cosine, sine):
    layout, arrays = split_pieces(pieces)
    rows, depth = arrays[0].shape
    length = 8 * rows
    parts, tall, _ = weight.shape
    width = tall // 4
    count = len(arrays)
    half_rot = ROT // 2

    def body(pos_ref, w_ref, b_ref, c_ref, s_ref, *refs):
        piece_refs = refs[:count]
        out_ref, hold, w_hold, made, sems, w_sems, o_sems = refs[count:]
        w_copies = weight_copies(w_ref, 3 * width, w_hold, w_sems)
        for copy in w_copies:
            copy.start()
        copies = start_pieces(layout, piece_refs, rows, hold, sems)
        for copy in w_copies:
            copy.wait()
        kept = []
        for core_step in range(2):
            wait_core(core_step, copies)
            for chunk in range(4 * core_step, 4 * core_step + 4):
                block = hold[chunk * rows : (chunk + 1) * rows, :]
                lanes = chunk_lanes(pos_ref, chunk, rows)
                cosines, sines = c_ref[:, lanes], s_ref[:, lanes]
                for kind in range(3):
                    band = slice(kind * width, (kind + 1) * width)
                    turned = dot_nt(w_hold[band, :], block) + b_ref[band, :]
                    if kind < 2:
                        bands = []
                        for first in range(0, width, HEAD_DIM):
                            r_one = turned[first : first + half_rot]
                            r_two = turned[first + half_rot : first + ROT]
                            bands.append(r_one * cosines - r_two * sines)
                            bands.append(r_two * cosines + r_one * sines)
                            bands.append(turned[first + ROT : first + HEAD_DIM])
                        turned = jnp.concatenate(bands, axis=0)
                    if kind == 0:
                        turned = turned * (1.0 / math.sqrt(HEAD_DIM))
                    made[chunk, band, :] = turned.astype(BF16)
            for chunk in range(4 * core_step, 4 * core_step + 4):
                copy = pltpu.make_async_copy(
                    made.at[chunk],
                    out_ref.at[:, chunk_lanes(pos_ref, chunk, rows)],
                    o_sems.at[chunk],
                )
                copy.start()
                kept.append(copy)
        for copy in kept:
            copy.wait()

    return pl.pallas_call(
        body,
        in_specs=[SM, ANY, VM, VM, VM] + [ANY] * count,
        out_specs=ANY,
        out_shape=jax.ShapeDtypeStruct((3 * width, length), BF16),
        scratch_shapes=[
            pltpu.VMEM((length, depth), BF16),
            pltpu.VMEM((3 * width, depth), BF16),
            pltpu.VMEM((8, 3 * width, rows), BF16),
            pltpu.SemaphoreType.DMA((count,)),
            pltpu.SemaphoreType.DMA((parts,)),
            pltpu.SemaphoreType.DMA((8,)),
        ],
        compiler_params=params(),
        cost_estimate=cost(6 * length * depth * width, 15 * MIB),
        name="project",
    )(pos, weight, bias, cosine, sine, *arrays)


def feed(pieces, weight):
    layout, arrays = split_pieces(pieces)
    rows, depth = arrays[0].shape
    length = 8 * rows
    parts, pair_units, _ = weight.shape
    units = pair_units // 2
    count = len(arrays)

    def body(w_ref, *refs):
        piece_refs = refs[:count]
        hid_ref, slope_ref, hold, w_hold, hid, slope = refs[count : count + 6]
        sems, w_sems, h_sems, s_sems = refs[count + 6 :]
        w_copies = weight_copies(w_ref, pair_units, w_hold, w_sems)
        for copy in w_copies:
            copy.start()
        copies = start_pieces(layout, piece_refs, rows, hold, sems)
        for copy in w_copies:
            copy.wait()
        kept = []
        for core_step in range(2):
            wait_core(core_step, copies)
            for chunk in range(4 * core_step, 4 * core_step + 4):
                here = slice(chunk * rows, (chunk + 1) * rows)
                block = hold[here, :]
                gate = dot_nt(w_hold[:units, :], block)
                up = dot_nt(w_hold[units:, :], block)
                sig = 0.5 + 0.5 * jnp.tanh(0.5 * gate)
                silu = gate * sig
                hid[:, here] = (silu * up).astype(BF16)
                slope[:units, here] = (up * (sig + silu * (1.0 - sig))).astype(BF16)
                slope[units:, here] = silu.astype(BF16)
            there = pl.ds(core_step * 4 * rows, 4 * rows)
            for made, out, o_sems in ((hid, hid_ref, h_sems), (slope, slope_ref, s_sems)):
                copy = pltpu.make_async_copy(
                    made.at[:, there], out.at[:, there], o_sems.at[core_step]
                )
                copy.start()
                kept.append(copy)
        for copy in kept:
            copy.wait()

    return pl.pallas_call(
        body,
        in_specs=[ANY] * (count + 1),
        out_specs=[ANY, ANY],
        out_shape=[
            jax.ShapeDtypeStruct((units, length), BF16),
            jax.ShapeDtypeStruct((pair_units, length), BF16),
        ],
        scratch_shapes=[
            pltpu.VMEM((length, depth), BF16),
            pltpu.VMEM((pair_units, depth), BF16),
            pltpu.VMEM((units, length), BF16),
            pltpu.VMEM((pair_units, length), BF16),
            pltpu.SemaphoreType.DMA((count,)),
            pltpu.SemaphoreType.DMA((parts,)),
            pltpu.SemaphoreType.DMA((2,)),
            pltpu.SemaphoreType.DMA((2,)),
        ],
        compiler_params=params(),
        cost_estimate=cost(2 * length * depth * pair_units, 22 * MIB),
        name="feed",
    )(weight, *arrays)


def feed_back(pieces, w_down, slopes, w_gate_up):
    pieces = [pieces[number] for number in (5, 6, 7, 8, 9, 0, 1, 2, 3, 4)]
    layout, arrays = split_pieces(pieces)
    rows, depth = arrays[0].shape
    parts, pair_units, cols = w_gate_up.shape
    units = pair_units // 2
    count = len(arrays)
    half = 4 * rows

    def body(wd_ref, s_ref, wg_ref, *refs):
        piece_refs = refs[:count]
        dgu_ref, o_ref, hold, w_hold, slope, wg_hold, made = refs[count : count + 7]
        sems, w_sems, s_sems, wg_sems, d_sems, o_sems = refs[count + 7 :]
        w_copies = weight_copies(wd_ref, units, w_hold, w_sems)
        for copy in w_copies:
            copy.start()
        copies = start_pieces(layout, piece_refs, rows, hold, sems)
        s_copies = []
        for core_step in (1, 0):
            there = pl.ds(core_step * half, half)
            copy = pltpu.make_async_copy(
                s_ref.at[:, there], slope.at[:, there], s_sems.at[core_step]
            )
            copy.start()
            s_copies.append(copy)
        wg_copies = [
            pltpu.make_async_copy(wg_ref.at[part], wg_hold.at[part], wg_sems.at[part])
            for part in range(parts)
        ]
        for copy in wg_copies:
            copy.start()
        for copy in w_copies:
            copy.wait()
        kept = []
        for core_step in (1, 0):
            wait_core(core_step, copies)
            s_copies[1 - core_step].wait()
            for chunk in range(4 * core_step, 4 * core_step + 4):
                here = slice(chunk * rows, (chunk + 1) * rows)
                d_hid = dot_nt(w_hold[...], hold[here, :])
                low = slope[:units, here].astype(F32)
                high = slope[units:, here].astype(F32)
                slope[:units, here] = (d_hid * low).astype(BF16)
                slope[units:, here] = (d_hid * high).astype(BF16)
            there = pl.ds(core_step * half, half)
            copy = pltpu.make_async_copy(
                slope.at[:, there], dgu_ref.at[:, there], d_sems.at[core_step]
            )
            copy.start()
            kept.append(copy)
        for copy in wg_copies:
            copy.wait()
        left = slope[:, half:].T
        for group in range(2):
            columns = pl.ds(group * depth // 2, depth // 2)
            for part in range(group * parts // 2, (group + 1) * parts // 2):
                made[:, part * cols : (part + 1) * cols] = dot_nn(left, wg_hold[part]).astype(BF16)
            copy = pltpu.make_async_copy(
                made.at[:, columns], o_ref.at[:, columns], o_sems.at[group]
            )
            copy.start()
            kept.append(copy)
        for copy in kept:
            copy.wait()

    return pl.pallas_call(
        body,
        in_specs=[ANY] * (count + 3),
        out_specs=[ANY, ANY],
        out_shape=[
            jax.ShapeDtypeStruct((pair_units, 2 * half), BF16),
            jax.ShapeDtypeStruct((half, depth), BF16),
        ],
        scratch_shapes=[
            pltpu.VMEM((2 * half, depth), BF16),
            pltpu.VMEM((units, depth), BF16),
            pltpu.VMEM((pair_units, 2 * half), BF16),
            pltpu.VMEM((parts, pair_units, cols), BF16),
            pltpu.VMEM((half, depth), BF16),
            pltpu.SemaphoreType.DMA((count,)),
            pltpu.SemaphoreType.DMA((parts,)),
            pltpu.SemaphoreType.DMA((2,)),
            pltpu.SemaphoreType.DMA((parts,)),
            pltpu.SemaphoreType.DMA((2,)),
            pltpu.SemaphoreType.DMA((2,)),
        ],
        compiler_params=params(),
        cost_estimate=cost(0, 0),
        name="feed_back",
    )(w_down, slopes, w_gate_up, *arrays)


def unit_grads(pieces, left, parts, name, scale=1):
    layout, arrays = split_pieces(pieces)
    rows, depth = arrays[0].shape
    height, length = left.shape
    cols = depth // parts
    count = len(arrays)

    def body(l_ref, *refs):
        piece_refs = refs[:count]
        out_ref, hold, sems = refs[count:]
        step = pl.program_id(0)
        copy_columns(step, parts, cols, layout, piece_refs, rows, hold, sems)
        columns = pl.ds(pl.multiple_of(step * cols, cols), cols)
        out_ref[0] = dot_nn(l_ref[...], hold[:, columns]).astype(BF16)

    return pl.pallas_call(
        body,
        grid=(parts,),
        in_specs=[pl.BlockSpec((height, length), lambda i: (0, 0), pipeline_mode=pl.Buffered(1))]
        + [ANY] * count,
        out_specs=pl.BlockSpec((1, height, cols), lambda i: (i, 0, 0)),
        out_shape=jax.ShapeDtypeStruct((parts, height, cols), BF16),
        scratch_shapes=[
            pltpu.VMEM((length, depth), BF16),
            pltpu.SemaphoreType.DMA((parts, count)),
        ],
        compiler_params=params(),
        cost_estimate=cost(2 * height * length * depth, 20 * MIB, scale),
        name=name,
    )(left, *arrays)


def rows_scratch(half, units, parts, cols):
    return [
        pltpu.VMEM((parts, units, cols), BF16),
        pltpu.VMEM((half, parts * cols), BF16),
        pltpu.SemaphoreType.DMA,
        pltpu.SemaphoreType.DMA((parts,)),
        pltpu.SemaphoreType.DMA((2,)),
    ]


def rows_of(left_copy, left, w_ref, units, o_ref, w_hold, made, w_sems, o_sems):
    parts, _, cols = w_ref.shape
    w_copies = [
        pltpu.make_async_copy(w_ref.at[part, pl.ds(0, units)], w_hold.at[part], w_sems.at[part])
        for part in range(parts)
    ]
    for copy in w_copies:
        copy.start()
    left_copy.wait()
    block = left()
    kept = []
    for group in range(2):
        members = range(group * parts // 2, (group + 1) * parts // 2)
        for part in members:
            w_copies[part].wait()
        for part in members:
            made[:, part * cols : (part + 1) * cols] = dot_nn(block, w_hold[part]).astype(BF16)
        columns = pl.ds(members.start * cols, len(members) * cols)
        copy = pltpu.make_async_copy(made.at[:, columns], o_ref.at[:, columns], o_sems.at[group])
        copy.start()
        kept.append(copy)
    for copy in kept:
        copy.wait()


def unit_rows(left, weight, core_step, name, scale=1):
    units, length = left.shape
    half = length // 2
    parts, _, cols = weight.shape

    def body(h_ref, w_ref, o_ref, held, w_hold, made, h_sem, w_sems, o_sems):
        h_copy = pltpu.make_async_copy(h_ref.at[:, pl.ds(core_step * half, half)], held, h_sem)
        h_copy.start()
        rows_of(h_copy, lambda: held[...].T, w_ref, units, o_ref, w_hold, made, w_sems, o_sems)

    return pl.pallas_call(
        body,
        in_specs=[ANY, ANY],
        out_specs=ANY,
        out_shape=jax.ShapeDtypeStruct((half, parts * cols), BF16),
        scratch_shapes=[pltpu.VMEM((units, half), BF16)]
        + rows_scratch(half, units, parts, cols),
        compiler_params=params(),
        cost_estimate=cost(2 * half * units * parts * cols, 9 * MIB, scale),
        name=name,
    )(left, weight)


def qkv_rows(pos, d_projected, weight, core_step, scale=1):
    tall, length = d_projected.shape
    rows = length // 8
    parts, _, cols = weight.shape

    def body(pos_ref, l_ref, w_ref, o_ref, held, w_hold, made, h_sem, w_sems, o_sems):
        for number in range(4):
            pltpu.make_async_copy(
                l_ref.at[:, chunk_lanes(pos_ref, 4 * core_step + number, rows)],
                held.at[:, pl.ds(number * rows, rows)],
                h_sem,
            ).start()
        h_copy = pltpu.make_async_copy(l_ref.at[:, pl.ds(0, 4 * rows)], held, h_sem)
        rows_of(h_copy, lambda: held[...].T, w_ref, tall, o_ref, w_hold, made, w_sems, o_sems)

    return pl.pallas_call(
        body,
        in_specs=[SM, ANY, ANY],
        out_specs=ANY,
        out_shape=jax.ShapeDtypeStruct((4 * rows, parts * cols), BF16),
        scratch_shapes=[pltpu.VMEM((tall, 4 * rows), BF16)]
        + rows_scratch(4 * rows, tall, parts, cols),
        compiler_params=params(),
        cost_estimate=cost(8 * rows * tall * parts * cols, 9 * MIB, scale),
        name="d_one_rows_sibling" if core_step else "d_one_rows_own",
    )(pos, d_projected, weight)


def attention_grads(pos, token_pieces, branch_pieces, d_projected, attended, parts):
    x_layout, x_arrays = split_pieces(token_pieces)
    b_layout, b_arrays = split_pieces(branch_pieces)
    rows, depth = x_arrays[0].shape
    width, length = attended.shape
    cols = depth // parts
    x_count, b_count = len(x_arrays), len(b_arrays)

    def body(pos_ref, dp_ref, a_ref, *refs):
        x_refs = refs[:x_count]
        b_refs = refs[x_count : x_count + b_count]
        o_ref, x_hold, b_hold, x_sems, b_sems = refs[x_count + b_count :]
        step = pl.program_id(0)
        columns = pl.ds(pl.multiple_of(step * cols, cols), cols)
        copy_columns(step, parts, cols, x_layout, x_refs, rows, x_hold, x_sems, pos_ref)
        copy_columns(step, parts, cols, b_layout, b_refs, rows, b_hold, b_sems, pos_ref)
        grad = dot_nn(dp_ref[...], x_hold[:, columns])
        for kind in range(3):
            o_ref[0, kind] = grad[kind * width : (kind + 1) * width].T.astype(BF16)
        o_ref[0, 3] = dot_nn(a_ref[...], b_hold[:, columns]).T.astype(BF16)

    whole = pl.Buffered(1)
    return pl.pallas_call(
        body,
        grid_spec=pltpu.PrefetchScalarGridSpec(
            num_scalar_prefetch=1,
            grid=(parts,),
            in_specs=[
                pl.BlockSpec((3 * width, length), lambda i, p: (0, 0), pipeline_mode=whole),
                pl.BlockSpec((width, length), lambda i, p: (0, 0), pipeline_mode=whole),
            ]
            + [ANY] * (x_count + b_count),
            out_specs=pl.BlockSpec((1, 4, cols, width), lambda i, p: (i, 0, 0, 0)),
            scratch_shapes=[
                pltpu.VMEM((length, depth), BF16),
                pltpu.VMEM((length, depth), BF16),
                pltpu.SemaphoreType.DMA((parts, x_count)),
                pltpu.SemaphoreType.DMA((parts, b_count)),
            ],
        ),
        out_shape=jax.ShapeDtypeStruct((parts, 4, cols, width), BF16),
        compiler_params=params(),
        cost_estimate=cost(8 * width * length * depth, 24 * MIB, 0.1),
        name="attention_grads",
    )(pos, d_projected, attended, *x_arrays, *b_arrays)


def chunk_lanes(pos_ref, chunk, rows):
    return pl.ds(pl.multiple_of(pos_ref[chunk] * rows, rows), rows)


def allowed_pairs(first_ref, q_at, k_at, size):
    lanes = pl.ds(pl.multiple_of(q_at * size, size), size)
    k_index = k_at * size + lax.broadcasted_iota(jnp.int32, (size, size), 0)
    q_index = q_at * size + lax.broadcasted_iota(jnp.int32, (size, size), 1)
    return (k_index >= first_ref[:, lanes]) & (k_index <= q_index)


def attend(pos, qkv, doc_first, start_block, size):
    length = qkv.shape[1]
    rows = length // 8
    width = qkv.shape[0] // 3
    heads = width // HEAD_DIM

    def body(pos_ref, start_ref, qkv_ref, first_ref, out_ref, log_ref, *refs):
        block_refs, held, acc = refs[:5], refs[5], refs[6]

        def query_block(q_at, _):
            q_lanes = pl.ds(pl.multiple_of(q_at * size, size), size)
            start = start_ref[q_at]
            every = range(heads)
            queries = [qkv_ref[h * HEAD_DIM : (h + 1) * HEAD_DIM, q_lanes] for h in every]

            def held_rows(k_at):
                return pl.ds(pl.multiple_of((k_at - start) * size, size), size)

            def find_top(k_at, tops):
                k_lanes = pl.ds(pl.multiple_of(k_at * size, size), size)
                mask = allowed_pairs(first_ref, q_at, k_at, size)
                new = []
                for head in every:
                    at = width + head * HEAD_DIM
                    logits = dot_tn(qkv_ref[at : at + HEAD_DIM, k_lanes], queries[head])
                    logits = jnp.where(mask, logits, -1e30)
                    held[head, held_rows(k_at), :] = logits
                    new.append(
                        jnp.maximum(
                            tops[head], jnp.max(logits.reshape(size // 8, 8, size), axis=0)
                        )
                    )
                return tuple(new)

            tops = lax.fori_loop(
                start,
                q_at + 1,
                find_top,
                tuple(jnp.full((8, size), -1e30, F32) for _ in every),
            )
            tops = [jnp.max(top, axis=0, keepdims=True) for top in tops]
            acc[...] = jnp.zeros_like(acc)

            def add_values(k_at, totals):
                k_lanes = pl.ds(pl.multiple_of(k_at * size, size), size)
                expons = []
                new = []
                for head in every:
                    expon = jnp.exp(held[head, held_rows(k_at), :] - tops[head])
                    new.append(
                        totals[head] + jnp.sum(expon.reshape(size // 8, 8, size), axis=0)
                    )
                    expons.append(expon.astype(BF16))
                outs = []
                for head in every:
                    at = 2 * width + head * HEAD_DIM
                    outs.append(dot_nn(qkv_ref[at : at + HEAD_DIM, k_lanes], expons[head]))
                acc[...] += jnp.concatenate(outs, axis=0)
                return tuple(new)

            totals = lax.fori_loop(
                start, q_at + 1, add_values, tuple(jnp.zeros((8, size), F32) for _ in every)
            )
            for head in every:
                total = jnp.sum(totals[head], axis=0, keepdims=True)
                band = slice(head * HEAD_DIM, (head + 1) * HEAD_DIM)
                out_ref[band, q_lanes] = (acc[band, :] / total).astype(BF16)
                log_ref[head : head + 1, q_lanes] = tops[head] + jnp.log(total)
            return 0

        lax.fori_loop(0, length // size, query_block, 0)
        for chunk in range(8):
            block = out_ref[:, chunk_lanes(pos_ref, chunk, rows)]
            if chunk < 4:
                block_refs[chunk][...] = block
            else:
                block_refs[4][chunk - 4] = block

    outs = pl.pallas_call(
        body,
        out_shape=[
            jax.ShapeDtypeStruct((width, length), BF16),
            jax.ShapeDtypeStruct((heads, length), F32),
        ]
        + [jax.ShapeDtypeStruct((width, rows), BF16)] * 4
        + [jax.ShapeDtypeStruct((4, width, rows), BF16)],
        in_specs=[SM, SM, VM, VM],
        out_specs=[VM] * 7,
        scratch_shapes=[
            pltpu.VMEM((heads, length, size), F32),
            pltpu.VMEM((width, size), F32),
        ],
        compiler_params=params(),
        cost_estimate=cost(0, 0),
        name="attend",
    )(pos, start_block, qkv, doc_first)
    return outs[0], outs[1], outs[2:6], outs[6]


def attend_back(
    pos, blocks, qkv, attended, log_sums, cosine, sine, doc_first, start_block, size
):
    width, length = attended.shape
    rows = length // 8
    heads = width // HEAD_DIM
    half_rot = ROT // 2
    scale = 1.0 / math.sqrt(HEAD_DIM)

    def body(pos_ref, start_ref, qkv_ref, att_ref, log_ref, c_ref, s_ref, first_ref, *refs):
        block_refs = refs[:5]
        out_ref, bias_ref, d_att, grads, sems = refs[5:]
        copies = exchanged_copies(
            block_refs, lambda chunk: d_att.at[:, chunk_lanes(pos_ref, chunk, rows)], sems
        )
        for copy in copies:
            copy.start()
        grads[...] = jnp.zeros_like(grads)
        for copy in copies:
            copy.wait()

        def query_block(q_at, _):
            q_lanes = pl.ds(pl.multiple_of(q_at * size, size), size)
            deltas = []
            for head in range(heads):
                at = head * HEAD_DIM
                deltas.append(
                    jnp.sum(
                        d_att[at : at + HEAD_DIM, q_lanes].astype(F32)
                        * att_ref[at : at + HEAD_DIM, q_lanes].astype(F32),
                        axis=0,
                        keepdims=True,
                    )
                )

            def key_block(k_at, _):
                k_lanes = pl.ds(pl.multiple_of(k_at * size, size), size)
                mask = allowed_pairs(first_ref, q_at, k_at, size)
                made = []
                for head in range(heads):
                    at = head * HEAD_DIM
                    key_at, value_at = width + at, 2 * width + at
                    query = qkv_ref[at : at + HEAD_DIM, q_lanes]
                    key = qkv_ref[key_at : key_at + HEAD_DIM, k_lanes]
                    value = qkv_ref[value_at : value_at + HEAD_DIM, k_lanes]
                    d_out = d_att[at : at + HEAD_DIM, q_lanes]
                    logits = dot_tn(key, query)
                    prob = jnp.where(
                        mask, jnp.exp(logits - log_ref[head : head + 1, q_lanes]), 0.0
                    )
                    d_prob = dot_tn(value, d_out)
                    d_logits = (prob * (d_prob - deltas[head])).astype(BF16)
                    made.append((query, key, d_out, d_logits, prob.astype(BF16)))
                for head in range(heads):
                    at = head * HEAD_DIM
                    key_at, value_at = width + at, 2 * width + at
                    query, key, d_out, d_logits, prob = made[head]
                    grads[at : at + HEAD_DIM, q_lanes] += dot_nn(key, d_logits)
                    grads[key_at : key_at + HEAD_DIM, k_lanes] += dot_nt(query, d_logits)
                    grads[value_at : value_at + HEAD_DIM, k_lanes] += dot_nt(d_out, prob)
                return 0

            lax.fori_loop(start_ref[q_at], q_at + 1, key_block, 0)
            return 0

        lax.fori_loop(0, length // size, query_block, 0)

        bias_ref[...] = jnp.zeros_like(bias_ref)

        def finish(at, _):
            lanes = pl.ds(pl.multiple_of(at * rows, rows), rows)
            cosines, sines = c_ref[:, lanes], s_ref[:, lanes]
            for kind in range(3):
                band = grads[kind * width : (kind + 1) * width, lanes]
                if kind == 0:
                    band = band * scale
                if kind < 2:
                    bands = []
                    for first in range(0, width, HEAD_DIM):
                        g_one = band[first : first + half_rot]
                        g_two = band[first + half_rot : first + ROT]
                        bands.append(g_one * cosines + g_two * sines)
                        bands.append(g_two * cosines - g_one * sines)
                        bands.append(band[first + ROT : first + HEAD_DIM])
                    band = jnp.concatenate(bands, axis=0)
                low = band.astype(BF16)
                out_ref[kind * width : (kind + 1) * width, lanes] = low
                bias_ref[kind * width : (kind + 1) * width, :] += jnp.sum(
                    low.astype(F32), axis=1, keepdims=True
                )
            return 0

        lax.fori_loop(0, length // rows, finish, 0)

    return pl.pallas_call(
        body,
        out_shape=[
            jax.ShapeDtypeStruct((3 * width, length), BF16),
            jax.ShapeDtypeStruct((3 * width, 1), F32),
        ],
        in_specs=[SM, SM] + [VM] * 6 + [ANY] * 5,
        out_specs=[VM, VM],
        scratch_shapes=[
            pltpu.VMEM((width, length), BF16),
            pltpu.VMEM((3 * width, length), F32),
            pltpu.SemaphoreType.DMA((8,)),
        ],
        compiler_params=params(),
        cost_estimate=cost(0, 0),
        name="attend_back",
    )(
        pos,
        start_block,
        qkv,
        attended,
        log_sums,
        cosine,
        sine,
        doc_first,
        *blocks,
    )


def doc_tables(doc_lengths, seq_length):
    doc_ends = jnp.cumsum(doc_lengths)
    doc_starts = doc_ends - doc_lengths
    places = jnp.arange(seq_length, dtype=jnp.int32)
    segment = jnp.sum((places[:, None] >= doc_ends[None, :-1]).astype(jnp.int32), axis=1)
    owners = segment[:, None] == jnp.arange(doc_lengths.shape[0], dtype=jnp.int32)[None, :]
    return places, jnp.sum(jnp.where(owners, doc_starts[None, :], 0), axis=1)


def shards(
    tokens,
    lengths,
    ln1_gain,
    ln1_bias,
    qkv_weight,
    qkv_bias,
    out_weight,
    ln2_gain,
    ln2_bias,
    gate_up_weight,
    down_weight,
    cotangent,
    axes,
):
    x = tokens[0]
    cot = cotangent[0]
    rows, depth = x.shape
    length = 8 * rows
    parts = axes["gx"]
    part_rows = depth // parts
    width = qkv_weight.shape[2]
    units = gate_up_weight.shape[2]
    size = 256
    gain_one = ln1_gain.astype(F32)[None]
    shift_one = ln1_bias.astype(F32)[None]
    gain_two = ln2_gain.astype(F32)[None]
    shift_two = ln2_bias.astype(F32)[None]

    attn_weight = jnp.concatenate(
        [qkv_weight.transpose(1, 2, 0).reshape(3 * width, part_rows), out_weight.T], axis=0
    )
    w_attn = lax.all_gather(attn_weight, "gx", axis=0, tiled=False)
    w_gate_up = lax.all_gather(
        gate_up_weight.transpose(1, 2, 0).reshape(2 * units, part_rows), "gx", axis=0, tiled=False
    )
    w_down = lax.all_gather(down_weight.T, "gx", axis=0, tiled=False)

    steps = jnp.arange(8, dtype=jnp.int32)
    pos = (lax.axis_index("gy") ^ (steps % 4)) * 2 + (lax.axis_index("gz") ^ (steps // 4))
    places, doc_first = doc_tables(lengths[0], length)
    start_block = doc_first[:: size] // size
    frequency = jnp.exp(
        jnp.arange(ROT // 2, dtype=F32) * (-2.0 * math.log(10000.0) / ROT)
    )
    angles = frequency[:, None] * (places - doc_first).astype(F32)[None, :]
    cosine, sine = jnp.cos(angles), jnp.sin(angles)
    doc_first = doc_first[None]

    bias_column = qkv_bias.astype(F32).reshape(3 * width, 1)
    normed_one = norm_one(x, gain_one, shift_one)
    one_pieces = gather_plane(normed_one, bias_column, cosine, sine, doc_first, start_block)
    cot_block = after(cot, one_pieces[1][0], one_pieces[2][0])
    cot_pieces = gather_plane(cot_block)
    out_block = w_attn[:, 3 * width :].transpose(1, 0, 2).reshape(width, depth)
    out_first = gather_first(out_block)
    qkv = project(
        pos,
        one_pieces,
        w_attn,
        after(bias_column, cot_pieces[3][0], cot_pieces[4][0], out_block),
        cosine,
        sine,
    )
    qkv = after(qkv, out_first[1], out_first[2], *[piece for piece, _, _ in cot_pieces])
    attended, log_sums, *blocks = attend(pos, qkv, doc_first, start_block, size)
    exchanged = []

    def exchange(*arrived):
        exchanged.extend(exchange_second(*exchange_first(*after(tuple(blocks), *arrived))))
        return exchanged[2:]

    out_pieces = gather_second(out_first, (qkv,), exchange)
    blocks = exchanged
    middle, normed_two = middle_norm(
        after(x, *[piece for piece, _, _ in cot_pieces]), blocks, out_pieces, gain_two, shift_two
    )

    two_pieces = gather_plane(normed_two)
    hidden, slopes = feed(two_pieces, w_gate_up)
    down_grad = unit_grads(cot_pieces, hidden, parts, "down_grads")
    down_grad_sum = lax.psum_scatter(down_grad, "gx", scatter_dimension=0, tiled=False)
    d_gate_up, d_two_sib = feed_back(cot_pieces, w_down, after(slopes, down_grad), w_gate_up)
    d_two_own = unit_rows(after(d_gate_up, d_two_sib), w_gate_up, 0, "d_two_rows_own", 0.3)
    came, sent = scatter_first(d_two_own, d_two_sib, rows)
    gate_up_grad = unit_grads(two_pieces, after(d_gate_up, *sent), parts, "gate_up_grads", 0.05)
    gate_up_grad_sum = lax.psum_scatter(gate_up_grad, "gx", scatter_dimension=0, tiled=False)
    sent, arrived = scatter_second(d_two_own, came, sent, rows, gate_up_grad, down_grad_sum)
    mlp_sib = unit_rows(
        after(hidden, gate_up_grad, *sent), w_down, 1, "mlp_rows_sibling", 0.1
    )
    d_two = scatter_last(d_two_own, came, sent, arrived)

    d_branch, norm_two_sums, d_middle, own_blocks, other_blocks = norm_two_back(
        after(middle, mlp_sib), cot, d_two, gain_two, out_pieces
    )
    blocks = exchange_second(*exchange_first(own_blocks, other_blocks))
    d_projected, bias_sums = attend_back(
        pos, blocks, qkv, attended, log_sums, cosine, sine, doc_first, start_block, size
    )
    branch_pieces = gather_plane(after(d_branch, *blocks[2:]), d_projected)
    d_one_sib = qkv_rows(
        pos, after(d_projected, branch_pieces[1][0], branch_pieces[2][0]), w_attn, 1, 0.1
    )
    d_one_own = qkv_rows(pos, after(d_projected, d_one_sib), w_attn, 0, 0.1)
    came, sent = scatter_first(d_one_own, d_one_sib, rows)
    attn_grads = attention_grads(
        pos, one_pieces, branch_pieces, d_projected, after(attended, *sent), parts
    )
    attn_grads_sum = lax.psum_scatter(attn_grads, "gx", scatter_dimension=0, tiled=False)
    sent, arrived = scatter_second(d_one_own, came, sent, rows, attn_grads)
    mlp_own = unit_rows(after(hidden, *sent), w_down, 0, "mlp_rows_own")
    mlp_came, mlp_sent = scatter_first(mlp_own, after(mlp_sib, *sent), rows)
    d_one = scatter_last(d_one_own, came, sent, arrived)
    gate_up_out = gate_up_grad_sum.astype(F32).reshape(2, units, part_rows).transpose(2, 0, 1)
    down_out = down_grad_sum.astype(F32).T
    input_grad, norm_one_sums = norm_one_back(
        after(x, gate_up_out, down_out), d_middle, d_one, gain_one
    )

    mlp_sent = after(mlp_sent, input_grad)
    mlp_sent, mlp_arrived = scatter_second(mlp_own, mlp_came, mlp_sent, rows)
    mlp = scatter_last(mlp_own, mlp_came, mlp_sent, mlp_arrived)
    half = rows // 2
    total = mlp[0][:rows].astype(F32) + mlp[1][:rows].astype(F32)
    total = total + jnp.concatenate(
        [
            mlp[2][half:].astype(F32) + mlp[4].astype(F32),
            mlp[3].astype(F32) + mlp[5][half:].astype(F32),
        ],
        axis=0,
    )
    activations = (middle + total).astype(BF16)

    bias_row = jnp.pad(bias_sums.reshape(1, 3 * width), ((0, 0), (0, depth - 3 * width)))
    small = jnp.concatenate([norm_one_sums, norm_two_sums, bias_row], axis=0)
    small = sum_all(small, [("gx", axes["gx"])])
    bias_sum = small[4, : 3 * width].reshape(3, width)
    norm_sums = sum_all(small[:4], [("gz", axes["gz"]), ("gy", axes["gy"])])
    attn_grads_sum = after(attn_grads_sum, activations, norm_sums, bias_sum).astype(F32)
    return (
        activations[None],
        input_grad[None],
        norm_sums[0],
        norm_sums[1],
        attn_grads_sum[:3].transpose(1, 0, 2),
        bias_sum,
        attn_grads_sum[3],
        norm_sums[2],
        norm_sums[3],
        gate_up_out,
        down_out,
    )


def solution(mesh):
    axes = dict(mesh.shape)
    placed = (
        P("gx", ("gy", "gz"), None),
        P("gx", None),
        P(),
        P(),
        P("gx", None, ("gy", "gz")),
        P(None, ("gy", "gz")),
        P("gx", ("gy", "gz")),
        P(),
        P(),
        P("gx", None, ("gy", "gz")),
        P("gx", ("gy", "gz")),
        P("gx", ("gy", "gz"), None),
    )
    return jax.shard_map(
        lambda *args: shards(*args, axes),
        mesh=mesh,
        in_specs=placed,
        out_specs=(
            P("gx", ("gy", "gz"), None),
            P("gx", ("gy", "gz"), None),
            P(),
            P(),
            P("gx", None, ("gy", "gz")),
            P(None, ("gy", "gz")),
            P("gx", ("gy", "gz")),
            P(),
            P(),
            P("gx", None, ("gy", "gz")),
            P("gx", ("gy", "gz")),
        ),
        check_vma=False,
    )
```

```python
import math

import jax
import jax.numpy as jnp
from jax import lax
from jax.experimental import pallas as pl
from jax.experimental.pallas import tpu as pltpu
from jax.sharding import PartitionSpec as P

HEAD_DIM = 64
ROT = 16
BF16 = jnp.bfloat16
F32 = jnp.float32
MIB = 1024 * 1024
SCALE = 1.0

SWAP_X = [(0, 1), (1, 0), (2, 3), (3, 2)]
SWAP_Y = [(0, 2), (2, 0), (1, 3), (3, 1)]
SWAP_FAR = [(0, 3), (3, 0), (1, 2), (2, 1)]
SWAP_CORE = [(0, 1), (1, 0)]


def to_x(values):
    return lax.ppermute(values, "gy", SWAP_X)


def to_y(values):
    return lax.ppermute(values, "gy", SWAP_Y)


def to_far(values):
    return lax.ppermute(values, "gy", SWAP_FAR)


def after(values, *others):
    return lax.optimization_barrier((values, others))[0]


def to_core(values):
    return lax.ppermute(values, "gz", SWAP_CORE)


def dot_nn(left, right):
    return lax.dot_general(left, right, (((1,), (0,)), ((), ())), preferred_element_type=F32)


def dot_nt(left, right):
    return lax.dot_general(left, right, (((1,), (1,)), ((), ())), preferred_element_type=F32)


def dot_tn(left, right):
    return lax.dot_general(left, right, (((0,), (0,)), ((), ())), preferred_element_type=F32)


def dot_tt(left, right):
    return lax.dot_general(left, right, (((0,), (1,)), ((), ())), preferred_element_type=F32)


VM = pl.BlockSpec(memory_space=pltpu.VMEM)
SM = pl.BlockSpec(memory_space=pltpu.SMEM)
ANY = pl.BlockSpec(memory_space=pl.ANY)


def params():
    return pltpu.CompilerParams(vmem_limit_bytes=58 * MIB)


def cost(flops, moved, scale=1):
    return pl.CostEstimate(
        flops=int(flops * scale * SCALE), bytes_accessed=int(moved * scale * SCALE), transcendentals=0
    )


def gather_first(block):
    return block, to_x(block), to_y(block), to_core(block)


def gather_plane(block, *between):
    return gather_second(gather_first(block), between)


def gather_second(first, between, later=None):
    block, from_x, from_y, other = first
    half = block.shape[0] // 2
    far_top = to_x(after(from_y[:half], *between))
    far_bottom = to_y(after(from_x[half:], *between))
    own = [(block, 0, 0), (from_x, 1, 0), (from_y, 2, 0), (far_top, 3, 0), (far_bottom, 3, half)]
    if later is not None:
        held = later(far_top, far_bottom)
        from_x, from_y, far_top, far_bottom = after((from_x, from_y, far_top, far_bottom), *held)
    return own + [
        (other, 4, 0),
        (to_core(from_x), 5, 0),
        (to_core(from_y), 6, 0),
        (to_core(far_top), 7, 0),
        (to_core(far_bottom), 7, half),
    ]


def exchange_plane(blocks):
    got = [blocks[0], to_x(blocks[1]), to_y(blocks[2]), to_far(blocks[3])]
    return got, to_core(jnp.stack([block[1] for block in got]))


def exchanged_copies(refs, hold_of, sems):
    copies = []
    for step in range(4):
        copies.append(pltpu.make_async_copy(refs[step].at[0], hold_of(step), sems.at[step]))
        copies.append(
            pltpu.make_async_copy(refs[4].at[step], hold_of(step + 4), sems.at[step + 4])
        )
    return copies


def scatter_first(own, sibling, rows):
    half = rows // 2
    came = to_core(sibling)

    def part(chunk, first):
        at = chunk * rows + first
        return (own[at : at + half].astype(F32) + came[at : at + half].astype(F32)).astype(BF16)

    for_x = jnp.concatenate([part(3, 0), part(1, 0)], axis=0)
    for_y = jnp.concatenate([part(3, half), part(2, half)], axis=0)
    return came, lax.optimization_barrier((for_x, for_y))


def scatter_second(own, came, sent, rows, *between):
    half = rows // 2
    from_x, from_y = after((to_x(sent[0]), to_y(sent[1])), *between)

    def part(chunk, first, more):
        at = chunk * rows + first
        total = own[at : at + half].astype(F32) + came[at : at + half].astype(F32)
        return (total + more.astype(F32)).astype(BF16)

    return [part(2, 0, from_x[:half]), part(1, half, from_y[:half])], [from_x, from_y]


def scatter_last(own, came, sent, arrived):
    y_top, x_bottom = to_y(sent[0]), to_x(sent[1])
    return own, came, arrived[0], x_bottom, y_top, arrived[1]


def summed(own_ref, came_ref, from_x, x_bottom, y_top, from_y):
    half = x_bottom.shape[0]
    total = own_ref[...].astype(F32) + came_ref[...].astype(F32)
    top = total[:half] + from_x[...].astype(F32) + y_top[...].astype(F32)
    bottom = total[half:] + x_bottom[...].astype(F32) + from_y[...].astype(F32)
    return jnp.concatenate([top, bottom], axis=0)


def sum_all(vectors, axes):
    for name, size in axes:
        step = 1
        while step < size:
            width = min(4, size // step)
            shifted = [
                lax.ppermute(vectors, name, [(i, i ^ (step * k)) for i in range(size)])
                for k in range(1, width)
            ]
            for other in shifted:
                vectors = vectors + other
            step *= width
    return vectors


def norm_parts(values):
    average = jnp.mean(values, axis=-1, keepdims=True)
    centered = values - average
    variance = jnp.mean(centered * centered, axis=-1, keepdims=True)
    rstd = lax.rsqrt(variance + 1e-05)
    return centered * rstd, rstd


def norm_one(tokens, gain, shift):
    def body(t_ref, g_ref, b_ref, o_ref):
        xhat, _ = norm_parts(t_ref[...].astype(F32))
        o_ref[...] = (xhat * g_ref[...] + b_ref[...]).astype(BF16)

    return pl.pallas_call(
        body,
        out_shape=jax.ShapeDtypeStruct(tokens.shape, BF16),
        in_specs=[VM] * 3,
        out_specs=VM,
        compiler_params=params(),
        cost_estimate=cost(0, 4 * tokens.size),
        name="norm_one",
    )(tokens, gain, shift)


def middle_norm(tokens, blocks, weight_pieces, gain, shift):
    rows, depth = tokens.shape
    layout, arrays = split_pieces(weight_pieces)
    width = blocks[0].shape[1]
    count = len(arrays)

    def body(t_ref, g_ref, b_ref, *refs):
        piece_refs = refs[:count]
        block_refs = refs[count : count + 5]
        m_ref, o_ref, hold, att, sems, b_sems = refs[count + 5 :]
        copies = exchanged_copies(
            block_refs, lambda chunk: att.at[pl.ds(chunk * width, width), :], b_sems
        )
        for copy in copies:
            copy.start()
        copies += [copy for _, copy in start_pieces(layout, piece_refs, width, hold, sems)]
        for copy in copies:
            copy.wait()
        middle = t_ref[...].astype(F32) + dot_tn(att[...], hold[...])
        m_ref[...] = middle
        xhat, _ = norm_parts(middle)
        o_ref[...] = (xhat * g_ref[...] + b_ref[...]).astype(BF16)

    return pl.pallas_call(
        body,
        out_shape=[
            jax.ShapeDtypeStruct((rows, depth), F32),
            jax.ShapeDtypeStruct((rows, depth), BF16),
        ],
        in_specs=[VM, VM, VM] + [ANY] * (count + 5),
        out_specs=[VM, VM],
        scratch_shapes=[
            pltpu.VMEM((8 * width, depth), BF16),
            pltpu.VMEM((8 * width, rows), BF16),
            pltpu.SemaphoreType.DMA((count,)),
            pltpu.SemaphoreType.DMA((8,)),
        ],
        compiler_params=params(),
        cost_estimate=cost(2 * rows * depth * 8 * width, 14 * MIB),
        name="middle_norm",
    )(tokens, gain, shift, *arrays, *blocks)


def norm_back_parts(v_ref, u_ref, part_refs, g_ref):
    e = summed(*part_refs)
    xhat, rstd = norm_parts(v_ref[...].astype(F32))
    d_xhat = e * g_ref[...]
    mean_d = jnp.mean(d_xhat, axis=-1, keepdims=True)
    mean_x = jnp.mean(d_xhat * xhat, axis=-1, keepdims=True)
    d_v = rstd * (d_xhat - mean_d - xhat * mean_x)
    sums = jnp.concatenate(
        [jnp.sum(e * xhat, axis=0, keepdims=True), jnp.sum(e, axis=0, keepdims=True)], axis=0
    )
    return u_ref[...].astype(F32) + d_v, sums


def norm_two_back(middle, cotangent, parts, gain, weight_pieces):
    rows, depth = middle.shape
    layout, arrays = split_pieces(weight_pieces)
    width = arrays[0].shape[0]
    count = len(arrays)

    def body(v_ref, u_ref, *refs):
        g_ref = refs[6]
        piece_refs = refs[7 : 7 + count]
        low_ref, sum_ref, wide_ref, *out_refs, hold, sems = refs[7 + count :]
        copies = start_pieces(layout, piece_refs, width, hold, sems)
        total, sum_ref[...] = norm_back_parts(v_ref, u_ref, refs[:6], g_ref)
        wide_ref[...] = total
        low_ref[...] = total.astype(BF16)
        for _, copy in copies:
            copy.wait()
        for chunk in range(8):
            block = dot_nt(hold[chunk * width : (chunk + 1) * width, :], low_ref[...]).astype(BF16)
            out_refs[chunk % 4][chunk // 4] = block

    whole = pl.BlockSpec((rows, depth), lambda i: (0, 0))
    line = pl.BlockSpec((1, depth), lambda i: (0, 0))
    two = pl.BlockSpec((2, depth), lambda i: (0, 0))
    half = pl.BlockSpec((rows // 2, depth), lambda i: (0, 0))
    second = pl.BlockSpec((rows // 2, depth), lambda i: (1, 0))
    block = pl.BlockSpec((2, width, rows), lambda i: (0, 0, 0))
    outs = pl.pallas_call(
        body,
        grid=(1,),
        in_specs=[whole, whole, whole, whole, second, half, half, second, line] + [ANY] * count,
        out_specs=[whole, two, whole] + [block] * 4,
        scratch_shapes=[
            pltpu.VMEM((8 * width, depth), BF16),
            pltpu.SemaphoreType.DMA((count,)),
        ],
        out_shape=[
            jax.ShapeDtypeStruct((rows, depth), BF16),
            jax.ShapeDtypeStruct((2, depth), F32),
            jax.ShapeDtypeStruct((rows, depth), F32),
        ]
        + [jax.ShapeDtypeStruct((2, width, rows), BF16)] * 4,
        compiler_params=params(),
        cost_estimate=cost(0, 0),
        name="norm_two_back",
    )(middle, cotangent, *parts, gain, *arrays)
    return outs[0], outs[1], outs[2], outs[3:]


def norm_one_back(tokens, d_middle, parts, gain):
    rows, depth = tokens.shape

    def body(v_ref, u_ref, *refs):
        g_ref, low_ref, sum_ref = refs[6:]
        total, sum_ref[...] = norm_back_parts(v_ref, u_ref, refs[:6], g_ref)
        low_ref[...] = total.astype(BF16)

    whole = pl.BlockSpec((rows, depth), lambda i: (0, 0))
    line = pl.BlockSpec((1, depth), lambda i: (0, 0))
    two = pl.BlockSpec((2, depth), lambda i: (0, 0))
    half = pl.BlockSpec((rows // 2, depth), lambda i: (0, 0))
    second = pl.BlockSpec((rows // 2, depth), lambda i: (1, 0))
    return pl.pallas_call(
        body,
        grid=(1,),
        out_shape=[
            jax.ShapeDtypeStruct((rows, depth), BF16),
            jax.ShapeDtypeStruct((2, depth), F32),
        ],
        in_specs=[whole, whole, whole, whole, second, half, half, second, line],
        out_specs=[whole, two],
        compiler_params=params(),
        cost_estimate=cost(0, 0),
        name="norm_one_back",
    )(tokens, d_middle, *parts, gain)


def split_pieces(pieces):
    return [(chunk, first) for _, chunk, first in pieces], [piece for piece, _, _ in pieces]


def start_pieces(layout, piece_refs, rows, hold, sems, pos_ref=None):
    copies = []
    for number, ((chunk, first), ref) in enumerate(zip(layout, piece_refs)):
        if pos_ref is None:
            at = chunk * rows + first
        else:
            at = pl.multiple_of(pos_ref[chunk] * rows + first, 16)
        copy = pltpu.make_async_copy(ref, hold.at[pl.ds(at, ref.shape[0]), :], sems.at[number])
        copy.start()
        copies.append((chunk, copy))
    return copies


def column_copies(part, cols, layout, piece_refs, rows, hold, sems, pos_ref=None):
    columns = pl.ds(part * cols, cols)
    copies = []
    for number, ((chunk, first), ref) in enumerate(zip(layout, piece_refs)):
        if pos_ref is None:
            at = chunk * rows + first
        else:
            at = pl.multiple_of(pos_ref[chunk] * rows + first, 16)
        copies.append(
            pltpu.make_async_copy(
                ref.at[:, columns],
                hold.at[pl.ds(at, ref.shape[0]), columns],
                sems.at[part, number],
            )
        )
    return copies


def weight_copies(w_ref, height, w_hold, w_sems):
    parts, _, cols = w_ref.shape
    return [
        pltpu.make_async_copy(
            w_ref.at[part, pl.ds(0, height)],
            w_hold.at[:, pl.ds(part * cols, cols)],
            w_sems.at[part],
        )
        for part in range(parts)
    ]


def wait_core(core_step, copies):
    for chunk, copy in copies:
        if chunk // 4 == core_step:
            copy.wait()


def project(pos, pieces, weight, bias, cosine, sine):
    layout, arrays = split_pieces(pieces)
    rows, depth = arrays[0].shape
    length = 8 * rows
    parts, tall, _ = weight.shape
    width = tall // 4
    count = len(arrays)
    half_rot = ROT // 2

    def body(pos_ref, w_ref, b_ref, c_ref, s_ref, *refs):
        piece_refs = refs[:count]
        out_ref, hold, w_hold, made, sems, w_sems, o_sems = refs[count:]
        w_copies = weight_copies(w_ref, 3 * width, w_hold, w_sems)
        for copy in w_copies:
            copy.start()
        copies = start_pieces(layout, piece_refs, rows, hold, sems)
        for copy in w_copies:
            copy.wait()
        kept = []
        for core_step in range(2):
            wait_core(core_step, copies)
            for chunk in range(4 * core_step, 4 * core_step + 4):
                block = hold[chunk * rows : (chunk + 1) * rows, :]
                lanes = chunk_lanes(pos_ref, chunk, rows)
                cosines, sines = c_ref[:, lanes], s_ref[:, lanes]
                for kind in range(3):
                    band = slice(kind * width, (kind + 1) * width)
                    turned = dot_nt(w_hold[band, :], block) + b_ref[band, :]
                    if kind < 2:
                        bands = []
                        for first in range(0, width, HEAD_DIM):
                            r_one = turned[first : first + half_rot]
                            r_two = turned[first + half_rot : first + ROT]
                            bands.append(r_one * cosines - r_two * sines)
                            bands.append(r_two * cosines + r_one * sines)
                            bands.append(turned[first + ROT : first + HEAD_DIM])
                        turned = jnp.concatenate(bands, axis=0)
                    if kind == 0:
                        turned = turned * (1.0 / math.sqrt(HEAD_DIM))
                    made[chunk, band, :] = turned.astype(BF16)
            for chunk in range(4 * core_step, 4 * core_step + 4):
                copy = pltpu.make_async_copy(
                    made.at[chunk],
                    out_ref.at[:, chunk_lanes(pos_ref, chunk, rows)],
                    o_sems.at[chunk],
                )
                copy.start()
                kept.append(copy)
        for copy in kept:
            copy.wait()

    return pl.pallas_call(
        body,
        in_specs=[SM, ANY, VM, VM, VM] + [ANY] * count,
        out_specs=ANY,
        out_shape=jax.ShapeDtypeStruct((3 * width, length), BF16),
        scratch_shapes=[
            pltpu.VMEM((length, depth), BF16),
            pltpu.VMEM((3 * width, depth), BF16),
            pltpu.VMEM((8, 3 * width, rows), BF16),
            pltpu.SemaphoreType.DMA((count,)),
            pltpu.SemaphoreType.DMA((parts,)),
            pltpu.SemaphoreType.DMA((8,)),
        ],
        compiler_params=params(),
        cost_estimate=cost(6 * length * depth * width, 15 * MIB),
        name="project",
    )(pos, weight, bias, cosine, sine, *arrays)


def feed(pieces, weight):
    layout, arrays = split_pieces(pieces)
    rows, depth = arrays[0].shape
    length = 8 * rows
    parts, pair_units, _ = weight.shape
    units = pair_units // 2
    count = len(arrays)

    def body(w_ref, *refs):
        piece_refs = refs[:count]
        hid_ref, slope_ref, hold, w_hold, hid, slope = refs[count : count + 6]
        sems, w_sems, h_sems, s_sems = refs[count + 6 :]
        w_copies = weight_copies(w_ref, pair_units, w_hold, w_sems)
        for copy in w_copies:
            copy.start()
        copies = start_pieces(layout, piece_refs, rows, hold, sems)
        for copy in w_copies:
            copy.wait()
        kept = []
        for core_step in range(2):
            wait_core(core_step, copies)
            for chunk in range(4 * core_step, 4 * core_step + 4):
                here = slice(chunk * rows, (chunk + 1) * rows)
                block = hold[here, :]
                gate = dot_nt(w_hold[:units, :], block)
                up = dot_nt(w_hold[units:, :], block)
                sig = 0.5 + 0.5 * jnp.tanh(0.5 * gate)
                silu = gate * sig
                hid[:, here] = (silu * up).astype(BF16)
                slope[:units, here] = (up * (sig + silu * (1.0 - sig))).astype(BF16)
                slope[units:, here] = silu.astype(BF16)
            there = pl.ds(core_step * 4 * rows, 4 * rows)
            for made, out, o_sems in ((hid, hid_ref, h_sems), (slope, slope_ref, s_sems)):
                copy = pltpu.make_async_copy(
                    made.at[:, there], out.at[:, there], o_sems.at[core_step]
                )
                copy.start()
                kept.append(copy)
        for copy in kept:
            copy.wait()

    return pl.pallas_call(
        body,
        in_specs=[ANY] * (count + 1),
        out_specs=[ANY, ANY],
        out_shape=[
            jax.ShapeDtypeStruct((units, length), BF16),
            jax.ShapeDtypeStruct((pair_units, length), BF16),
        ],
        scratch_shapes=[
            pltpu.VMEM((length, depth), BF16),
            pltpu.VMEM((pair_units, depth), BF16),
            pltpu.VMEM((units, length), BF16),
            pltpu.VMEM((pair_units, length), BF16),
            pltpu.SemaphoreType.DMA((count,)),
            pltpu.SemaphoreType.DMA((parts,)),
            pltpu.SemaphoreType.DMA((2,)),
            pltpu.SemaphoreType.DMA((2,)),
        ],
        compiler_params=params(),
        cost_estimate=cost(2 * length * depth * pair_units, 22 * MIB),
        name="feed",
    )(weight, *arrays)


def feed_back(pieces, w_down, slopes, w_gate_up, core_step, d_gate_up=None):
    pieces = [
        (piece, chunk - 4 * core_step, first)
        for piece, chunk, first in pieces
        if chunk // 4 == core_step
    ]
    layout, arrays = split_pieces(pieces)
    rows, depth = arrays[0].shape
    parts, pair_units, cols = w_gate_up.shape
    units = pair_units // 2
    count = len(arrays)
    half = 4 * rows
    given = [] if d_gate_up is None else [d_gate_up]

    def body(wd_ref, s_ref, wg_ref, *refs):
        piece_refs = refs[:count]
        refs = refs[count + len(given) :]
        dgu_ref, o_ref, hold, wd_hold, slope, w_hold, made = refs[:7]
        sems, wd_sems, s_sem, w_sems, d_sem, o_sems = refs[7:]
        there = pl.ds(core_step * half, half)
        wd_copies = weight_copies(wd_ref, units, wd_hold, wd_sems)
        for copy in wd_copies:
            copy.start()
        copies = start_pieces(layout, piece_refs, rows, hold, sems)
        s_copy = pltpu.make_async_copy(s_ref.at[:, there], slope, s_sem)
        s_copy.start()
        for copy in wd_copies:
            copy.wait()
        for _, copy in copies:
            copy.wait()
        kept = pltpu.make_async_copy(slope, dgu_ref.at[:, there], d_sem)

        def left():
            for chunk in range(4):
                here = slice(chunk * rows, (chunk + 1) * rows)
                d_hid = dot_nt(wd_hold[...], hold[here, :])
                low = slope[:units, here].astype(F32)
                high = slope[units:, here].astype(F32)
                slope[:units, here] = (d_hid * low).astype(BF16)
                slope[units:, here] = (d_hid * high).astype(BF16)
            kept.start()
            return slope[...].T

        rows_of(s_copy, left, wg_ref, pair_units, o_ref, w_hold, made, w_sems, o_sems)
        kept.wait()

    return pl.pallas_call(
        body,
        in_specs=[ANY] * (count + 3 + len(given)),
        out_specs=[ANY, ANY],
        out_shape=[
            jax.ShapeDtypeStruct((pair_units, 2 * half), BF16),
            jax.ShapeDtypeStruct((half, depth), BF16),
        ],
        scratch_shapes=[
            pltpu.VMEM((half, depth), BF16),
            pltpu.VMEM((units, depth), BF16),
            pltpu.VMEM((pair_units, half), BF16),
            pltpu.VMEM((parts, pair_units, cols), BF16),
            pltpu.VMEM((half, depth), BF16),
            pltpu.SemaphoreType.DMA((count,)),
            pltpu.SemaphoreType.DMA((parts,)),
            pltpu.SemaphoreType.DMA,
            pltpu.SemaphoreType.DMA((parts,)),
            pltpu.SemaphoreType.DMA,
            pltpu.SemaphoreType.DMA((2,)),
        ],
        input_output_aliases={3 + count: 0} if given else {},
        compiler_params=params(),
        cost_estimate=cost(2 * half * depth * units, 10 * MIB, 0.1),
        name="feed_back_sibling" if core_step else "feed_back_own",
    )(w_down, slopes, w_gate_up, *arrays, *given)


def grads_of(left, pieces, parts, name, pos=None, kinds=0, scale=1):
    layout, arrays = split_pieces(pieces)
    rows, depth = arrays[0].shape
    height, length = left.shape
    cols = depth // parts
    count = len(arrays)
    shape = (kinds, cols, height // kinds) if kinds else (height, cols)

    def body(pos_ref, l_ref, *refs):
        piece_refs = refs[:count]
        out_ref, l_hold, hold, made, l_sem, sems, o_sems = refs[count:]
        l_copy = pltpu.make_async_copy(l_ref, l_hold, l_sem)
        l_copy.start()
        order = None if pos is None else pos_ref
        groups = [
            column_copies(group, depth // 2, layout, piece_refs, rows, hold, sems, order)
            for group in range(2)
        ]
        for group in groups:
            for copy in group:
                copy.start()
        l_copy.wait()
        kept = []
        for group in range(2):
            for copy in groups[group]:
                copy.wait()
            members = range(group * parts // 2, (group + 1) * parts // 2)
            for part in members:
                grad = dot_nn(l_hold[...], hold[:, part * cols : (part + 1) * cols])
                if kinds:
                    for kind in range(kinds):
                        band = grad[kind * shape[2] : (kind + 1) * shape[2]]
                        made[part, kind] = band.T.astype(BF16)
                else:
                    made[part] = grad.astype(BF16)
            there = pl.ds(members.start, len(members))
            copy = pltpu.make_async_copy(made.at[there], out_ref.at[there], o_sems.at[group])
            copy.start()
            kept.append(copy)
        for copy in kept:
            copy.wait()

    return pl.pallas_call(
        body,
        in_specs=[SM] + [ANY] * (count + 1),
        out_specs=ANY,
        out_shape=jax.ShapeDtypeStruct((parts, *shape), BF16),
        scratch_shapes=[
            pltpu.VMEM((height, length), BF16),
            pltpu.VMEM((length, depth), BF16),
            pltpu.VMEM((parts, *shape), BF16),
            pltpu.SemaphoreType.DMA,
            pltpu.SemaphoreType.DMA((2, count)),
            pltpu.SemaphoreType.DMA((2,)),
        ],
        compiler_params=params(),
        cost_estimate=cost(2 * height * length * depth, 20 * MIB, scale),
        name=name,
    )(jnp.zeros((8,), jnp.int32) if pos is None else pos, left, *arrays)


def rows_scratch(half, units, parts, cols):
    return [
        pltpu.VMEM((parts, units, cols), BF16),
        pltpu.VMEM((half, parts * cols), BF16),
        pltpu.SemaphoreType.DMA,
        pltpu.SemaphoreType.DMA((parts,)),
        pltpu.SemaphoreType.DMA((2,)),
    ]


def rows_of(left_copy, left, w_ref, units, o_ref, w_hold, made, w_sems, o_sems):
    parts, _, cols = w_ref.shape
    w_copies = [
        pltpu.make_async_copy(w_ref.at[part, pl.ds(0, units)], w_hold.at[part], w_sems.at[part])
        for part in range(parts)
    ]
    for copy in w_copies:
        copy.start()
    left_copy.wait()
    block = left()
    kept = []
    for group in range(2):
        members = range(group * parts // 2, (group + 1) * parts // 2)
        for part in members:
            w_copies[part].wait()
        for part in members:
            made[:, part * cols : (part + 1) * cols] = dot_nn(block, w_hold[part]).astype(BF16)
        columns = pl.ds(members.start * cols, len(members) * cols)
        copy = pltpu.make_async_copy(made.at[:, columns], o_ref.at[:, columns], o_sems.at[group])
        copy.start()
        kept.append(copy)
    for copy in kept:
        copy.wait()


def unit_rows(left, weight, core_step, name, scale=1):
    units, length = left.shape
    half = length // 2
    parts, _, cols = weight.shape

    def body(h_ref, w_ref, o_ref, held, w_hold, made, h_sem, w_sems, o_sems):
        h_copy = pltpu.make_async_copy(h_ref.at[:, pl.ds(core_step * half, half)], held, h_sem)
        h_copy.start()
        rows_of(h_copy, lambda: held[...].T, w_ref, units, o_ref, w_hold, made, w_sems, o_sems)

    return pl.pallas_call(
        body,
        in_specs=[ANY, ANY],
        out_specs=ANY,
        out_shape=jax.ShapeDtypeStruct((half, parts * cols), BF16),
        scratch_shapes=[pltpu.VMEM((units, half), BF16)]
        + rows_scratch(half, units, parts, cols),
        compiler_params=params(),
        cost_estimate=cost(2 * half * units * parts * cols, 9 * MIB, scale),
        name=name,
    )(left, weight)


def qkv_rows(pos, d_projected, weight, core_step, scale=1):
    tall, length = d_projected.shape
    rows = length // 8
    parts, _, cols = weight.shape

    def body(pos_ref, l_ref, w_ref, o_ref, held, w_hold, made, h_sem, w_sems, o_sems):
        for number in range(4):
            pltpu.make_async_copy(
                l_ref.at[:, chunk_lanes(pos_ref, 4 * core_step + number, rows)],
                held.at[:, pl.ds(number * rows, rows)],
                h_sem,
            ).start()
        h_copy = pltpu.make_async_copy(l_ref.at[:, pl.ds(0, 4 * rows)], held, h_sem)
        rows_of(h_copy, lambda: held[...].T, w_ref, tall, o_ref, w_hold, made, w_sems, o_sems)

    return pl.pallas_call(
        body,
        in_specs=[SM, ANY, ANY],
        out_specs=ANY,
        out_shape=jax.ShapeDtypeStruct((4 * rows, parts * cols), BF16),
        scratch_shapes=[pltpu.VMEM((tall, 4 * rows), BF16)]
        + rows_scratch(4 * rows, tall, parts, cols),
        compiler_params=params(),
        cost_estimate=cost(8 * rows * tall * parts * cols, 9 * MIB, scale),
        name="d_one_rows_sibling" if core_step else "d_one_rows_own",
    )(pos, d_projected, weight)


def chunk_lanes(pos_ref, chunk, rows):
    return pl.ds(pl.multiple_of(pos_ref[chunk] * rows, rows), rows)


def allowed_pairs(first_ref, q_at, k_at, size):
    lanes = pl.ds(pl.multiple_of(q_at * size, size), size)
    k_index = k_at * size + lax.broadcasted_iota(jnp.int32, (size, size), 0)
    q_index = q_at * size + lax.broadcasted_iota(jnp.int32, (size, size), 1)
    return (k_index >= first_ref[:, lanes]) & (k_index <= q_index)


def attend(pos, qkv, doc_first, start_block, size):
    length = qkv.shape[1]
    rows = length // 8
    width = qkv.shape[0] // 3
    heads = width // HEAD_DIM

    def body(pos_ref, start_ref, qkv_ref, first_ref, out_ref, log_ref, *refs):
        block_refs, held, acc = refs[:4], refs[4], refs[5]

        def query_block(q_at, _):
            q_lanes = pl.ds(pl.multiple_of(q_at * size, size), size)
            start = start_ref[q_at]
            every = range(heads)
            queries = [qkv_ref[h * HEAD_DIM : (h + 1) * HEAD_DIM, q_lanes] for h in every]

            def held_rows(k_at):
                return pl.ds(pl.multiple_of((k_at - start) * size, size), size)

            def find_top(k_at, tops):
                k_lanes = pl.ds(pl.multiple_of(k_at * size, size), size)
                mask = allowed_pairs(first_ref, q_at, k_at, size)
                new = []
                for head in every:
                    at = width + head * HEAD_DIM
                    logits = dot_tn(qkv_ref[at : at + HEAD_DIM, k_lanes], queries[head])
                    logits = jnp.where(mask, logits, -1e30)
                    held[head, held_rows(k_at), :] = logits
                    new.append(
                        jnp.maximum(
                            tops[head], jnp.max(logits.reshape(size // 8, 8, size), axis=0)
                        )
                    )
                return tuple(new)

            tops = lax.fori_loop(
                start,
                q_at + 1,
                find_top,
                tuple(jnp.full((8, size), -1e30, F32) for _ in every),
            )
            tops = [jnp.max(top, axis=0, keepdims=True) for top in tops]
            acc[...] = jnp.zeros_like(acc)

            def add_values(k_at, totals):
                k_lanes = pl.ds(pl.multiple_of(k_at * size, size), size)
                expons = []
                new = []
                for head in every:
                    expon = jnp.exp(held[head, held_rows(k_at), :] - tops[head])
                    new.append(
                        totals[head] + jnp.sum(expon.reshape(size // 8, 8, size), axis=0)
                    )
                    expons.append(expon.astype(BF16))
                outs = []
                for head in every:
                    at = 2 * width + head * HEAD_DIM
                    outs.append(dot_nn(qkv_ref[at : at + HEAD_DIM, k_lanes], expons[head]))
                acc[...] += jnp.concatenate(outs, axis=0)
                return tuple(new)

            totals = lax.fori_loop(
                start, q_at + 1, add_values, tuple(jnp.zeros((8, size), F32) for _ in every)
            )
            for head in every:
                total = jnp.sum(totals[head], axis=0, keepdims=True)
                band = slice(head * HEAD_DIM, (head + 1) * HEAD_DIM)
                out_ref[band, q_lanes] = (acc[band, :] / total).astype(BF16)
                log_ref[head : head + 1, q_lanes] = tops[head] + jnp.log(total)
            return 0

        lax.fori_loop(0, length // size, query_block, 0)
        for chunk in range(8):
            block = out_ref[:, chunk_lanes(pos_ref, chunk, rows)]
            block_refs[chunk % 4][chunk // 4] = block

    outs = pl.pallas_call(
        body,
        out_shape=[
            jax.ShapeDtypeStruct((width, length), BF16),
            jax.ShapeDtypeStruct((heads, length), F32),
        ]
        + [jax.ShapeDtypeStruct((2, width, rows), BF16)] * 4,
        in_specs=[SM, SM, VM, VM],
        out_specs=[VM] * 6,
        scratch_shapes=[
            pltpu.VMEM((heads, length, size), F32),
            pltpu.VMEM((width, size), F32),
        ],
        compiler_params=params(),
        cost_estimate=cost(0, 0),
        name="attend",
    )(pos, start_block, qkv, doc_first)
    return outs[0], outs[1], outs[2:]


def attend_back(
    pos, blocks, qkv, attended, log_sums, cosine, sine, doc_first, start_block, size
):
    width, length = attended.shape
    rows = length // 8
    heads = width // HEAD_DIM
    half_rot = ROT // 2
    scale = 1.0 / math.sqrt(HEAD_DIM)

    def body(pos_ref, start_ref, qkv_ref, att_ref, log_ref, c_ref, s_ref, first_ref, *refs):
        block_refs = refs[:5]
        out_ref, bias_ref, d_att, grads, sems = refs[5:]
        copies = exchanged_copies(
            block_refs, lambda chunk: d_att.at[:, chunk_lanes(pos_ref, chunk, rows)], sems
        )
        for copy in copies:
            copy.start()
        grads[...] = jnp.zeros_like(grads)
        for copy in copies:
            copy.wait()

        def query_block(q_at, _):
            q_lanes = pl.ds(pl.multiple_of(q_at * size, size), size)
            deltas = []
            for head in range(heads):
                at = head * HEAD_DIM
                deltas.append(
                    jnp.sum(
                        d_att[at : at + HEAD_DIM, q_lanes].astype(F32)
                        * att_ref[at : at + HEAD_DIM, q_lanes].astype(F32),
                        axis=0,
                        keepdims=True,
                    )
                )

            def key_block(k_at, _):
                k_lanes = pl.ds(pl.multiple_of(k_at * size, size), size)
                mask = allowed_pairs(first_ref, q_at, k_at, size)
                made = []
                for head in range(heads):
                    at = head * HEAD_DIM
                    key_at, value_at = width + at, 2 * width + at
                    query = qkv_ref[at : at + HEAD_DIM, q_lanes]
                    key = qkv_ref[key_at : key_at + HEAD_DIM, k_lanes]
                    value = qkv_ref[value_at : value_at + HEAD_DIM, k_lanes]
                    d_out = d_att[at : at + HEAD_DIM, q_lanes]
                    logits = dot_tn(key, query)
                    prob = jnp.where(
                        mask, jnp.exp(logits - log_ref[head : head + 1, q_lanes]), 0.0
                    )
                    d_prob = dot_tn(value, d_out)
                    d_logits = (prob * (d_prob - deltas[head])).astype(BF16)
                    made.append((query, key, d_out, d_logits, prob.astype(BF16)))
                for head in range(heads):
                    at = head * HEAD_DIM
                    key_at, value_at = width + at, 2 * width + at
                    query, key, d_out, d_logits, prob = made[head]
                    grads[at : at + HEAD_DIM, q_lanes] += dot_nn(key, d_logits)
                    grads[key_at : key_at + HEAD_DIM, k_lanes] += dot_nt(query, d_logits)
                    grads[value_at : value_at + HEAD_DIM, k_lanes] += dot_nt(d_out, prob)
                return 0

            lax.fori_loop(start_ref[q_at], q_at + 1, key_block, 0)
            return 0

        lax.fori_loop(0, length // size, query_block, 0)

        bias_ref[...] = jnp.zeros_like(bias_ref)

        def finish(at, _):
            lanes = pl.ds(pl.multiple_of(at * rows, rows), rows)
            cosines, sines = c_ref[:, lanes], s_ref[:, lanes]
            for kind in range(3):
                band = grads[kind * width : (kind + 1) * width, lanes]
                if kind == 0:
                    band = band * scale
                if kind < 2:
                    bands = []
                    for first in range(0, width, HEAD_DIM):
                        g_one = band[first : first + half_rot]
                        g_two = band[first + half_rot : first + ROT]
                        bands.append(g_one * cosines + g_two * sines)
                        bands.append(g_two * cosines - g_one * sines)
                        bands.append(band[first + ROT : first + HEAD_DIM])
                    band = jnp.concatenate(bands, axis=0)
                low = band.astype(BF16)
                out_ref[kind * width : (kind + 1) * width, lanes] = low
                bias_ref[kind * width : (kind + 1) * width, :] += jnp.sum(
                    low.astype(F32), axis=1, keepdims=True
                )
            return 0

        lax.fori_loop(0, length // rows, finish, 0)

    return pl.pallas_call(
        body,
        out_shape=[
            jax.ShapeDtypeStruct((3 * width, length), BF16),
            jax.ShapeDtypeStruct((3 * width, 1), F32),
        ],
        in_specs=[SM, SM] + [VM] * 6 + [ANY] * 5,
        out_specs=[VM, VM],
        scratch_shapes=[
            pltpu.VMEM((width, length), BF16),
            pltpu.VMEM((3 * width, length), F32),
            pltpu.SemaphoreType.DMA((8,)),
        ],
        compiler_params=params(),
        cost_estimate=cost(0, 0),
        name="attend_back",
    )(
        pos,
        start_block,
        qkv,
        attended,
        log_sums,
        cosine,
        sine,
        doc_first,
        *blocks,
    )


def doc_tables(doc_lengths, seq_length):
    doc_ends = jnp.cumsum(doc_lengths)
    doc_starts = doc_ends - doc_lengths
    places = jnp.arange(seq_length, dtype=jnp.int32)
    segment = jnp.sum((places[:, None] >= doc_ends[None, :-1]).astype(jnp.int32), axis=1)
    owners = segment[:, None] == jnp.arange(doc_lengths.shape[0], dtype=jnp.int32)[None, :]
    return places, jnp.sum(jnp.where(owners, doc_starts[None, :], 0), axis=1)


def shards(
    tokens,
    lengths,
    ln1_gain,
    ln1_bias,
    qkv_weight,
    qkv_bias,
    out_weight,
    ln2_gain,
    ln2_bias,
    gate_up_weight,
    down_weight,
    cotangent,
    axes,
):
    x = tokens[0]
    cot = cotangent[0]
    rows, depth = x.shape
    length = 8 * rows
    parts = axes["gx"]
    part_rows = depth // parts
    width = qkv_weight.shape[2]
    units = gate_up_weight.shape[2]
    size = 256
    gain_one = ln1_gain.astype(F32)[None]
    shift_one = ln1_bias.astype(F32)[None]
    gain_two = ln2_gain.astype(F32)[None]
    shift_two = ln2_bias.astype(F32)[None]

    attn_weight = jnp.concatenate(
        [qkv_weight.transpose(1, 2, 0).reshape(3 * width, part_rows), out_weight.T], axis=0
    )
    w_attn = lax.all_gather(attn_weight, "gx", axis=0, tiled=False)
    w_gate_up = lax.all_gather(
        gate_up_weight.transpose(1, 2, 0).reshape(2 * units, part_rows), "gx", axis=0, tiled=False
    )
    w_down = lax.all_gather(down_weight.T, "gx", axis=0, tiled=False)

    steps = jnp.arange(8, dtype=jnp.int32)
    pos = (lax.axis_index("gy") ^ (steps % 4)) * 2 + (lax.axis_index("gz") ^ (steps // 4))
    places, doc_first = doc_tables(lengths[0], length)
    start_block = doc_first[:: size] // size
    frequency = jnp.exp(
        jnp.arange(ROT // 2, dtype=F32) * (-2.0 * math.log(10000.0) / ROT)
    )
    angles = frequency[:, None] * (places - doc_first).astype(F32)[None, :]
    cosine, sine = jnp.cos(angles), jnp.sin(angles)
    doc_first = doc_first[None]

    bias_column = qkv_bias.astype(F32).reshape(3 * width, 1)
    normed_one = norm_one(x, gain_one, shift_one)
    one_pieces = gather_plane(normed_one, bias_column, cosine, sine, doc_first, start_block)
    cot_block = after(cot, one_pieces[1][0], one_pieces[2][0])
    cot_pieces = gather_plane(cot_block)
    out_block = w_attn[:, 3 * width :].transpose(1, 0, 2).reshape(width, depth)
    out_first = gather_first(out_block)
    qkv = project(
        pos,
        one_pieces,
        w_attn,
        after(bias_column, cot_pieces[3][0], cot_pieces[4][0], out_block),
        cosine,
        sine,
    )
    qkv = after(qkv, out_first[1], out_first[2], *[piece for piece, _, _ in cot_pieces])
    attended, log_sums, blocks = attend(pos, qkv, doc_first, start_block, size)
    exchanged = []

    def exchange(*arrived):
        got, other = exchange_plane(after(tuple(blocks), *arrived))
        exchanged.extend([*got, other])
        return exchanged[1:]

    out_pieces = gather_second(out_first, (qkv,), exchange)
    blocks = exchanged
    middle, normed_two = middle_norm(
        after(x, *[piece for piece, _, _ in cot_pieces]), blocks, out_pieces, gain_two, shift_two
    )

    two_pieces = gather_plane(normed_two)
    hidden, slopes = feed(two_pieces, w_gate_up)
    down_grad = grads_of(hidden, cot_pieces, parts, "down_grads", scale=0.1)
    down_grad_sum = lax.psum_scatter(down_grad, "gx", scatter_dimension=0, tiled=False)
    d_gate_up, d_two_sib = feed_back(cot_pieces, w_down, after(slopes, down_grad), w_gate_up, 1)
    d_gate_up, d_two_own = feed_back(
        cot_pieces, w_down, after(slopes, d_two_sib), w_gate_up, 0, d_gate_up
    )
    came, sent = scatter_first(d_two_own, d_two_sib, rows)
    gate_up_grad = grads_of(after(d_gate_up, *sent), two_pieces, parts, "gate_up_grads", scale=0.05)
    sent, arrived = scatter_second(d_two_own, came, sent, rows, gate_up_grad)
    gate_up_grad_sum = lax.psum_scatter(
        after(gate_up_grad, *sent), "gx", scatter_dimension=0, tiled=False
    )
    mlp_sib = unit_rows(
        after(hidden, gate_up_grad, *sent), w_down, 1, "mlp_rows_sibling", 0.1
    )
    d_two = scatter_last(d_two_own, came, sent, arrived)

    d_branch, norm_two_sums, d_middle, blocks = norm_two_back(
        after(middle, mlp_sib), cot, d_two, gain_two, out_pieces
    )
    got, other = exchange_plane(blocks)
    blocks = [*got, other]
    d_projected, bias_sums = attend_back(
        pos,
        blocks,
        qkv,
        after(attended, down_grad_sum),
        log_sums,
        cosine,
        sine,
        doc_first,
        start_block,
        size,
    )
    branch_pieces = gather_plane(after(d_branch, *blocks[1:]), d_projected)
    far_pieces = (branch_pieces[3][0], branch_pieces[4][0])
    qkv_grad = grads_of(
        after(d_projected, branch_pieces[1][0], branch_pieces[2][0]),
        one_pieces,
        parts,
        "qkv_grads",
        pos,
        kinds=3,
        scale=0,
    )
    qkv_grad = after(qkv_grad, *far_pieces)
    qkv_grad_sum = lax.psum_scatter(qkv_grad, "gx", scatter_dimension=0, tiled=False)
    d_one_sib = qkv_rows(pos, after(d_projected, qkv_grad), w_attn, 1, 0)
    d_one_own = qkv_rows(pos, after(d_projected, d_one_sib), w_attn, 0, 0)
    came, sent = scatter_first(d_one_own, d_one_sib, rows)
    out_grad = grads_of(
        after(attended, *sent), branch_pieces, parts, "out_grads", pos, kinds=1, scale=0
    )
    out_grad_sum = lax.psum_scatter(out_grad, "gx", scatter_dimension=0, tiled=False)
    mlp_own = unit_rows(after(hidden, out_grad), w_down, 0, "mlp_rows_own", 0)
    mlp_came, mlp_sent = scatter_first(mlp_own, after(mlp_sib, d_branch), rows)
    sent, arrived = scatter_second(d_one_own, came, sent, rows, *mlp_sent)
    d_one = scatter_last(d_one_own, came, sent, arrived)
    mlp_sent, mlp_arrived = scatter_second(mlp_own, mlp_came, after(mlp_sent, *sent), rows)

    mlp = scatter_last(mlp_own, mlp_came, mlp_sent, mlp_arrived)
    half = rows // 2
    total = mlp[0][:rows].astype(F32) + mlp[1][:rows].astype(F32)
    total = total + jnp.concatenate(
        [
            mlp[2][half:].astype(F32) + mlp[4].astype(F32),
            mlp[3].astype(F32) + mlp[5][half:].astype(F32),
        ],
        axis=0,
    )
    activations = (middle + total).astype(BF16)
    input_grad, norm_one_sums = norm_one_back(x, d_middle, d_one, gain_one)
    gate_up_grad_sum, down_grad_sum = after((gate_up_grad_sum, down_grad_sum), *mlp_sent)
    gate_up_out = gate_up_grad_sum.astype(F32).reshape(2, units, part_rows).transpose(2, 0, 1)
    down_out = down_grad_sum.astype(F32).T

    bias_row = jnp.pad(bias_sums.reshape(1, 3 * width), ((0, 0), (0, depth - 3 * width)))
    small = jnp.concatenate([norm_one_sums, norm_two_sums, bias_row], axis=0)
    small = sum_all(small, [("gx", axes["gx"])])
    bias_sum = small[4, : 3 * width].reshape(3, width)
    norm_sums = sum_all(small[:4], [("gz", axes["gz"]), ("gy", axes["gy"])])
    qkv_grad_sum, out_grad_sum = after(
        (qkv_grad_sum, out_grad_sum[0]), activations, norm_sums, bias_sum, gate_up_out, down_out
    )
    return (
        activations[None],
        input_grad[None],
        norm_sums[0],
        norm_sums[1],
        qkv_grad_sum.astype(F32).transpose(1, 0, 2),
        bias_sum,
        out_grad_sum.astype(F32),
        norm_sums[2],
        norm_sums[3],
        gate_up_out,
        down_out,
    )


def solution(mesh):
    axes = dict(mesh.shape)
    placed = (
        P("gx", ("gy", "gz"), None),
        P("gx", None),
        P(),
        P(),
        P("gx", None, ("gy", "gz")),
        P(None, ("gy", "gz")),
        P("gx", ("gy", "gz")),
        P(),
        P(),
        P("gx", None, ("gy", "gz")),
        P("gx", ("gy", "gz")),
        P("gx", ("gy", "gz"), None),
    )
    return jax.shard_map(
        lambda *args: shards(*args, axes),
        mesh=mesh,
        in_specs=placed,
        out_specs=(
            P("gx", ("gy", "gz"), None),
            P("gx", ("gy", "gz"), None),
            P(),
            P(),
            P("gx", None, ("gy", "gz")),
            P(None, ("gy", "gz")),
            P("gx", ("gy", "gz")),
            P(),
            P(),
            P("gx", None, ("gy", "gz")),
            P("gx", ("gy", "gz")),
        ),
        check_vma=False,
    )
```

```python
import math

import jax
import jax.numpy as jnp
from jax import lax
from jax.experimental import pallas as pl
from jax.experimental.pallas import tpu as pltpu
from jax.sharding import PartitionSpec as P

HEAD_DIM = 64
ROT = 16
BF16 = jnp.bfloat16
F32 = jnp.float32
MIB = 1024 * 1024
SCALE = 1.0

SWAP_X = [(0, 1), (1, 0), (2, 3), (3, 2)]
SWAP_Y = [(0, 2), (2, 0), (1, 3), (3, 1)]
SWAP_FAR = [(0, 3), (3, 0), (1, 2), (2, 1)]
SWAP_CORE = [(0, 1), (1, 0)]


def to_x(values):
    return lax.ppermute(values, "gy", SWAP_X)


def to_y(values):
    return lax.ppermute(values, "gy", SWAP_Y)


def to_far(values):
    return lax.ppermute(values, "gy", SWAP_FAR)


def after(values, *others):
    return lax.optimization_barrier((values, others))[0]


def to_core(values):
    return lax.ppermute(values, "gz", SWAP_CORE)


def dot_nn(left, right):
    return lax.dot_general(left, right, (((1,), (0,)), ((), ())), preferred_element_type=F32)


def dot_nt(left, right):
    return lax.dot_general(left, right, (((1,), (1,)), ((), ())), preferred_element_type=F32)


def dot_tn(left, right):
    return lax.dot_general(left, right, (((0,), (0,)), ((), ())), preferred_element_type=F32)


def dot_tt(left, right):
    return lax.dot_general(left, right, (((0,), (1,)), ((), ())), preferred_element_type=F32)


VM = pl.BlockSpec(memory_space=pltpu.VMEM)
SM = pl.BlockSpec(memory_space=pltpu.SMEM)
ANY = pl.BlockSpec(memory_space=pl.ANY)


def params():
    return pltpu.CompilerParams(vmem_limit_bytes=58 * MIB)


def cost(flops, moved, scale=1):
    return pl.CostEstimate(
        flops=int(flops * scale * SCALE), bytes_accessed=int(moved * scale * SCALE), transcendentals=0
    )


def gather_first(block):
    return block, to_x(block), to_y(block), to_core(block)


def gather_plane(block, *between):
    return gather_second(gather_first(block), between)


def gather_second(first, between, later=None):
    block, from_x, from_y, other = first
    half = block.shape[0] // 2
    far_top = to_x(after(from_y[:half], *between))
    far_bottom = to_y(after(from_x[half:], *between))
    own = [(block, 0, 0), (from_x, 1, 0), (from_y, 2, 0), (far_top, 3, 0), (far_bottom, 3, half)]
    if later is not None:
        held = later(far_top, far_bottom)
        from_x, from_y, far_top, far_bottom = after((from_x, from_y, far_top, far_bottom), *held)
    return own + [
        (other, 4, 0),
        (to_core(from_x), 5, 0),
        (to_core(from_y), 6, 0),
        (to_core(far_top), 7, 0),
        (to_core(far_bottom), 7, half),
    ]


def exchange_plane(blocks):
    got = [blocks[0], to_x(blocks[1]), to_y(blocks[2]), to_far(blocks[3])]
    return got, to_core(jnp.stack([block[1] for block in got]))


def exchanged_copies(refs, hold_of, sems):
    copies = []
    for step in range(4):
        copies.append(pltpu.make_async_copy(refs[step].at[0], hold_of(step), sems.at[step]))
        copies.append(
            pltpu.make_async_copy(refs[4].at[step], hold_of(step + 4), sems.at[step + 4])
        )
    return copies


def scatter_first(own, sibling, rows):
    half = rows // 2
    came = to_core(sibling)

    def part(chunk, first):
        at = chunk * rows + first
        return (own[at : at + half].astype(F32) + came[at : at + half].astype(F32)).astype(BF16)

    for_x = jnp.concatenate([part(3, 0), part(1, 0)], axis=0)
    for_y = jnp.concatenate([part(3, half), part(2, half)], axis=0)
    return came, lax.optimization_barrier((for_x, for_y))


def scatter_second(own, came, sent, rows, *between):
    half = rows // 2
    from_x, from_y = after((to_x(sent[0]), to_y(sent[1])), *between)

    def part(chunk, first, more):
        at = chunk * rows + first
        total = own[at : at + half].astype(F32) + came[at : at + half].astype(F32)
        return (total + more.astype(F32)).astype(BF16)

    return [part(2, 0, from_x[:half]), part(1, half, from_y[:half])], [from_x, from_y]


def scatter_last(own, came, sent, arrived):
    y_top, x_bottom = to_y(sent[0]), to_x(sent[1])
    return own, came, arrived[0], x_bottom, y_top, arrived[1]


def summed(own_ref, came_ref, from_x, x_bottom, y_top, from_y):
    half = x_bottom.shape[0]
    total = own_ref[...].astype(F32) + came_ref[...].astype(F32)
    top = total[:half] + from_x[...].astype(F32) + y_top[...].astype(F32)
    bottom = total[half:] + x_bottom[...].astype(F32) + from_y[...].astype(F32)
    return jnp.concatenate([top, bottom], axis=0)


def sum_all(vectors, axes):
    for name, size in axes:
        step = 1
        while step < size:
            width = min(4, size // step)
            shifted = [
                lax.ppermute(vectors, name, [(i, i ^ (step * k)) for i in range(size)])
                for k in range(1, width)
            ]
            for other in shifted:
                vectors = vectors + other
            step *= width
    return vectors


def norm_parts(values):
    average = jnp.mean(values, axis=-1, keepdims=True)
    centered = values - average
    variance = jnp.mean(centered * centered, axis=-1, keepdims=True)
    rstd = lax.rsqrt(variance + 1e-05)
    return centered * rstd, rstd


def norm_one(tokens, gain, shift):
    def body(t_ref, g_ref, b_ref, o_ref):
        xhat, _ = norm_parts(t_ref[...].astype(F32))
        o_ref[...] = (xhat * g_ref[...] + b_ref[...]).astype(BF16)

    return pl.pallas_call(
        body,
        out_shape=jax.ShapeDtypeStruct(tokens.shape, BF16),
        in_specs=[VM] * 3,
        out_specs=VM,
        compiler_params=params(),
        cost_estimate=cost(0, 4 * tokens.size),
        name="norm_one",
    )(tokens, gain, shift)


def middle_norm(tokens, blocks, weight_pieces, gain, shift):
    rows, depth = tokens.shape
    layout, arrays = split_pieces(weight_pieces)
    width = blocks[0].shape[1]
    count = len(arrays)

    def body(t_ref, g_ref, b_ref, *refs):
        piece_refs = refs[:count]
        block_refs = refs[count : count + 5]
        m_ref, o_ref, hold, att, sems, b_sems = refs[count + 5 :]
        copies = exchanged_copies(
            block_refs, lambda chunk: att.at[pl.ds(chunk * width, width), :], b_sems
        )
        for copy in copies:
            copy.start()
        copies += [copy for _, copy in start_pieces(layout, piece_refs, width, hold, sems)]
        for copy in copies:
            copy.wait()
        middle = t_ref[...].astype(F32) + dot_tn(att[...], hold[...])
        m_ref[...] = middle
        xhat, _ = norm_parts(middle)
        o_ref[...] = (xhat * g_ref[...] + b_ref[...]).astype(BF16)

    return pl.pallas_call(
        body,
        out_shape=[
            jax.ShapeDtypeStruct((rows, depth), F32),
            jax.ShapeDtypeStruct((rows, depth), BF16),
        ],
        in_specs=[VM, VM, VM] + [ANY] * (count + 5),
        out_specs=[VM, VM],
        scratch_shapes=[
            pltpu.VMEM((8 * width, depth), BF16),
            pltpu.VMEM((8 * width, rows), BF16),
            pltpu.SemaphoreType.DMA((count,)),
            pltpu.SemaphoreType.DMA((8,)),
        ],
        compiler_params=params(),
        cost_estimate=cost(2 * rows * depth * 8 * width, 14 * MIB),
        name="middle_norm",
    )(tokens, gain, shift, *arrays, *blocks)


def norm_back_parts(v_ref, u_ref, part_refs, g_ref):
    e = summed(*part_refs)
    xhat, rstd = norm_parts(v_ref[...].astype(F32))
    d_xhat = e * g_ref[...]
    mean_d = jnp.mean(d_xhat, axis=-1, keepdims=True)
    mean_x = jnp.mean(d_xhat * xhat, axis=-1, keepdims=True)
    d_v = rstd * (d_xhat - mean_d - xhat * mean_x)
    sums = jnp.concatenate(
        [jnp.sum(e * xhat, axis=0, keepdims=True), jnp.sum(e, axis=0, keepdims=True)], axis=0
    )
    return u_ref[...].astype(F32) + d_v, sums


def norm_two_back(middle, cotangent, parts, gain, weight_pieces):
    rows, depth = middle.shape
    layout, arrays = split_pieces(weight_pieces)
    width = arrays[0].shape[0]
    count = len(arrays)

    def body(v_ref, u_ref, *refs):
        g_ref = refs[6]
        piece_refs = refs[7 : 7 + count]
        low_ref, sum_ref, wide_ref, *out_refs, hold, sems = refs[7 + count :]
        copies = start_pieces(layout, piece_refs, width, hold, sems)
        total, sum_ref[...] = norm_back_parts(v_ref, u_ref, refs[:6], g_ref)
        wide_ref[...] = total
        low_ref[...] = total.astype(BF16)
        for _, copy in copies:
            copy.wait()
        for chunk in range(8):
            block = dot_nt(hold[chunk * width : (chunk + 1) * width, :], low_ref[...]).astype(BF16)
            out_refs[chunk % 4][chunk // 4] = block

    whole = pl.BlockSpec((rows, depth), lambda i: (0, 0))
    line = pl.BlockSpec((1, depth), lambda i: (0, 0))
    two = pl.BlockSpec((2, depth), lambda i: (0, 0))
    half = pl.BlockSpec((rows // 2, depth), lambda i: (0, 0))
    second = pl.BlockSpec((rows // 2, depth), lambda i: (1, 0))
    block = pl.BlockSpec((2, width, rows), lambda i: (0, 0, 0))
    outs = pl.pallas_call(
        body,
        grid=(1,),
        in_specs=[whole, whole, whole, whole, second, half, half, second, line] + [ANY] * count,
        out_specs=[whole, two, whole] + [block] * 4,
        scratch_shapes=[
            pltpu.VMEM((8 * width, depth), BF16),
            pltpu.SemaphoreType.DMA((count,)),
        ],
        out_shape=[
            jax.ShapeDtypeStruct((rows, depth), BF16),
            jax.ShapeDtypeStruct((2, depth), F32),
            jax.ShapeDtypeStruct((rows, depth), F32),
        ]
        + [jax.ShapeDtypeStruct((2, width, rows), BF16)] * 4,
        compiler_params=params(),
        cost_estimate=cost(0, 0),
        name="norm_two_back",
    )(middle, cotangent, *parts, gain, *arrays)
    return outs[0], outs[1], outs[2], outs[3:]


def norm_one_back(tokens, d_middle, parts, gain):
    rows, depth = tokens.shape

    def body(v_ref, u_ref, *refs):
        g_ref, low_ref, sum_ref = refs[6:]
        total, sum_ref[...] = norm_back_parts(v_ref, u_ref, refs[:6], g_ref)
        low_ref[...] = total.astype(BF16)

    whole = pl.BlockSpec((rows, depth), lambda i: (0, 0))
    line = pl.BlockSpec((1, depth), lambda i: (0, 0))
    two = pl.BlockSpec((2, depth), lambda i: (0, 0))
    half = pl.BlockSpec((rows // 2, depth), lambda i: (0, 0))
    second = pl.BlockSpec((rows // 2, depth), lambda i: (1, 0))
    return pl.pallas_call(
        body,
        grid=(1,),
        out_shape=[
            jax.ShapeDtypeStruct((rows, depth), BF16),
            jax.ShapeDtypeStruct((2, depth), F32),
        ],
        in_specs=[whole, whole, whole, whole, second, half, half, second, line],
        out_specs=[whole, two],
        compiler_params=params(),
        cost_estimate=cost(0, 0),
        name="norm_one_back",
    )(tokens, d_middle, *parts, gain)


def split_pieces(pieces):
    return [(chunk, first) for _, chunk, first in pieces], [piece for piece, _, _ in pieces]


def start_pieces(layout, piece_refs, rows, hold, sems, pos_ref=None):
    copies = []
    for number, ((chunk, first), ref) in enumerate(zip(layout, piece_refs)):
        if pos_ref is None:
            at = chunk * rows + first
        else:
            at = pl.multiple_of(pos_ref[chunk] * rows + first, 16)
        copy = pltpu.make_async_copy(ref, hold.at[pl.ds(at, ref.shape[0]), :], sems.at[number])
        copy.start()
        copies.append((chunk, copy))
    return copies


def column_copies(part, cols, layout, piece_refs, rows, hold, sems, pos_ref=None):
    columns = pl.ds(part * cols, cols)
    copies = []
    for number, ((chunk, first), ref) in enumerate(zip(layout, piece_refs)):
        if pos_ref is None:
            at = chunk * rows + first
        else:
            at = pl.multiple_of(pos_ref[chunk] * rows + first, 16)
        copies.append(
            pltpu.make_async_copy(
                ref.at[:, columns],
                hold.at[pl.ds(at, ref.shape[0]), columns],
                sems.at[part, number],
            )
        )
    return copies


def weight_copies(w_ref, height, w_hold, w_sems):
    parts, _, cols = w_ref.shape
    return [
        pltpu.make_async_copy(
            w_ref.at[part, pl.ds(0, height)],
            w_hold.at[:, pl.ds(part * cols, cols)],
            w_sems.at[part],
        )
        for part in range(parts)
    ]


def wait_core(core_step, copies):
    for chunk, copy in copies:
        if chunk // 4 == core_step:
            copy.wait()


def project(pos, pieces, weight, bias, cosine, sine):
    layout, arrays = split_pieces(pieces)
    rows, depth = arrays[0].shape
    length = 8 * rows
    parts, tall, _ = weight.shape
    width = tall // 4
    count = len(arrays)
    half_rot = ROT // 2

    def body(pos_ref, w_ref, b_ref, c_ref, s_ref, *refs):
        piece_refs = refs[:count]
        out_ref, hold, w_hold, made, sems, w_sems, o_sems = refs[count:]
        w_copies = weight_copies(w_ref, 3 * width, w_hold, w_sems)
        for copy in w_copies:
            copy.start()
        copies = start_pieces(layout, piece_refs, rows, hold, sems)
        for copy in w_copies:
            copy.wait()
        kept = []
        for core_step in range(2):
            wait_core(core_step, copies)
            for chunk in range(4 * core_step, 4 * core_step + 4):
                block = hold[chunk * rows : (chunk + 1) * rows, :]
                lanes = chunk_lanes(pos_ref, chunk, rows)
                cosines, sines = c_ref[:, lanes], s_ref[:, lanes]
                for kind in range(3):
                    band = slice(kind * width, (kind + 1) * width)
                    turned = dot_nt(w_hold[band, :], block) + b_ref[band, :]
                    if kind < 2:
                        bands = []
                        for first in range(0, width, HEAD_DIM):
                            r_one = turned[first : first + half_rot]
                            r_two = turned[first + half_rot : first + ROT]
                            bands.append(r_one * cosines - r_two * sines)
                            bands.append(r_two * cosines + r_one * sines)
                            bands.append(turned[first + ROT : first + HEAD_DIM])
                        turned = jnp.concatenate(bands, axis=0)
                    if kind == 0:
                        turned = turned * (1.0 / math.sqrt(HEAD_DIM))
                    made[chunk, band, :] = turned.astype(BF16)
            for chunk in range(4 * core_step, 4 * core_step + 4):
                copy = pltpu.make_async_copy(
                    made.at[chunk],
                    out_ref.at[:, chunk_lanes(pos_ref, chunk, rows)],
                    o_sems.at[chunk],
                )
                copy.start()
                kept.append(copy)
        for copy in kept:
            copy.wait()

    return pl.pallas_call(
        body,
        in_specs=[SM, ANY, VM, VM, VM] + [ANY] * count,
        out_specs=ANY,
        out_shape=jax.ShapeDtypeStruct((3 * width, length), BF16),
        scratch_shapes=[
            pltpu.VMEM((length, depth), BF16),
            pltpu.VMEM((3 * width, depth), BF16),
            pltpu.VMEM((8, 3 * width, rows), BF16),
            pltpu.SemaphoreType.DMA((count,)),
            pltpu.SemaphoreType.DMA((parts,)),
            pltpu.SemaphoreType.DMA((8,)),
        ],
        compiler_params=params(),
        cost_estimate=cost(6 * length * depth * width, 15 * MIB),
        name="project",
    )(pos, weight, bias, cosine, sine, *arrays)


def feed(pieces, weight):
    layout, arrays = split_pieces(pieces)
    rows, depth = arrays[0].shape
    length = 8 * rows
    parts, pair_units, _ = weight.shape
    units = pair_units // 2
    count = len(arrays)

    def body(w_ref, *refs):
        piece_refs = refs[:count]
        hid_ref, slope_ref, hold, w_hold, hid, slope = refs[count : count + 6]
        sems, w_sems, h_sems, s_sems = refs[count + 6 :]
        w_copies = weight_copies(w_ref, pair_units, w_hold, w_sems)
        for copy in w_copies:
            copy.start()
        copies = start_pieces(layout, piece_refs, rows, hold, sems)
        for copy in w_copies:
            copy.wait()
        kept = []
        for core_step in range(2):
            wait_core(core_step, copies)
            for chunk in range(4 * core_step, 4 * core_step + 4):
                here = slice(chunk * rows, (chunk + 1) * rows)
                block = hold[here, :]
                gate = dot_nt(w_hold[:units, :], block)
                up = dot_nt(w_hold[units:, :], block)
                sig = 0.5 + 0.5 * jnp.tanh(0.5 * gate)
                silu = gate * sig
                hid[:, here] = (silu * up).astype(BF16)
                slope[:units, here] = (up * (sig + silu * (1.0 - sig))).astype(BF16)
                slope[units:, here] = silu.astype(BF16)
            there = pl.ds(core_step * 4 * rows, 4 * rows)
            for made, out, o_sems in ((hid, hid_ref, h_sems), (slope, slope_ref, s_sems)):
                copy = pltpu.make_async_copy(
                    made.at[:, there], out.at[:, there], o_sems.at[core_step]
                )
                copy.start()
                kept.append(copy)
        for copy in kept:
            copy.wait()

    return pl.pallas_call(
        body,
        in_specs=[ANY] * (count + 1),
        out_specs=[ANY, ANY],
        out_shape=[
            jax.ShapeDtypeStruct((units, length), BF16),
            jax.ShapeDtypeStruct((pair_units, length), BF16),
        ],
        scratch_shapes=[
            pltpu.VMEM((length, depth), BF16),
            pltpu.VMEM((pair_units, depth), BF16),
            pltpu.VMEM((units, length), BF16),
            pltpu.VMEM((pair_units, length), BF16),
            pltpu.SemaphoreType.DMA((count,)),
            pltpu.SemaphoreType.DMA((parts,)),
            pltpu.SemaphoreType.DMA((2,)),
            pltpu.SemaphoreType.DMA((2,)),
        ],
        compiler_params=params(),
        cost_estimate=cost(2 * length * depth * pair_units, 22 * MIB),
        name="feed",
    )(weight, *arrays)


def feed_back(pieces, w_down, slopes, w_gate_up, core_step, d_gate_up=None):
    pieces = [
        (piece, chunk - 4 * core_step, first)
        for piece, chunk, first in pieces
        if chunk // 4 == core_step
    ]
    layout, arrays = split_pieces(pieces)
    rows, depth = arrays[0].shape
    parts, pair_units, cols = w_gate_up.shape
    units = pair_units // 2
    count = len(arrays)
    half = 4 * rows
    given = [] if d_gate_up is None else [d_gate_up]

    def body(wd_ref, s_ref, wg_ref, *refs):
        piece_refs = refs[:count]
        refs = refs[count + len(given) :]
        dgu_ref, o_ref, hold, wd_hold, slope, w_hold, made = refs[:7]
        sems, wd_sems, s_sem, w_sems, d_sem, o_sems = refs[7:]
        there = pl.ds(core_step * half, half)
        wd_copies = weight_copies(wd_ref, units, wd_hold, wd_sems)
        for copy in wd_copies:
            copy.start()
        copies = start_pieces(layout, piece_refs, rows, hold, sems)
        s_copy = pltpu.make_async_copy(s_ref.at[:, there], slope, s_sem)
        s_copy.start()
        for copy in wd_copies:
            copy.wait()
        for _, copy in copies:
            copy.wait()
        kept = pltpu.make_async_copy(slope, dgu_ref.at[:, there], d_sem)

        def left():
            for chunk in range(4):
                here = slice(chunk * rows, (chunk + 1) * rows)
                d_hid = dot_nt(wd_hold[...], hold[here, :])
                low = slope[:units, here].astype(F32)
                high = slope[units:, here].astype(F32)
                slope[:units, here] = (d_hid * low).astype(BF16)
                slope[units:, here] = (d_hid * high).astype(BF16)
            kept.start()
            return slope[...].T

        rows_of(s_copy, left, wg_ref, pair_units, o_ref, w_hold, made, w_sems, o_sems)
        kept.wait()

    return pl.pallas_call(
        body,
        in_specs=[ANY] * (count + 3 + len(given)),
        out_specs=[ANY, ANY],
        out_shape=[
            jax.ShapeDtypeStruct((pair_units, 2 * half), BF16),
            jax.ShapeDtypeStruct((half, depth), BF16),
        ],
        scratch_shapes=[
            pltpu.VMEM((half, depth), BF16),
            pltpu.VMEM((units, depth), BF16),
            pltpu.VMEM((pair_units, half), BF16),
            pltpu.VMEM((parts, pair_units, cols), BF16),
            pltpu.VMEM((half, depth), BF16),
            pltpu.SemaphoreType.DMA((count,)),
            pltpu.SemaphoreType.DMA((parts,)),
            pltpu.SemaphoreType.DMA,
            pltpu.SemaphoreType.DMA((parts,)),
            pltpu.SemaphoreType.DMA,
            pltpu.SemaphoreType.DMA((2,)),
        ],
        input_output_aliases={3 + count: 0} if given else {},
        compiler_params=params(),
        cost_estimate=cost(2 * half * depth * units, 10 * MIB, 0.1),
        name="feed_back_sibling" if core_step else "feed_back_own",
    )(w_down, slopes, w_gate_up, *arrays, *given)


def grads_of(left, pieces, parts, name, pos=None, kinds=0, scale=1):
    layout, arrays = split_pieces(pieces)
    rows, depth = arrays[0].shape
    height, length = left.shape
    cols = depth // parts
    count = len(arrays)
    shape = (kinds, cols, height // kinds) if kinds else (height, cols)

    def body(pos_ref, l_ref, *refs):
        piece_refs = refs[:count]
        out_ref, l_hold, hold, made, l_sem, sems, o_sems = refs[count:]
        l_copy = pltpu.make_async_copy(l_ref, l_hold, l_sem)
        l_copy.start()
        order = None if pos is None else pos_ref
        groups = [
            column_copies(group, depth // 2, layout, piece_refs, rows, hold, sems, order)
            for group in range(2)
        ]
        for group in groups:
            for copy in group:
                copy.start()
        l_copy.wait()
        kept = []
        for group in range(2):
            for copy in groups[group]:
                copy.wait()
            members = range(group * parts // 2, (group + 1) * parts // 2)
            for part in members:
                grad = dot_nn(l_hold[...], hold[:, part * cols : (part + 1) * cols])
                if kinds:
                    for kind in range(kinds):
                        band = grad[kind * shape[2] : (kind + 1) * shape[2]]
                        made[part, kind] = band.T.astype(BF16)
                else:
                    made[part] = grad.astype(BF16)
            there = pl.ds(members.start, len(members))
            copy = pltpu.make_async_copy(made.at[there], out_ref.at[there], o_sems.at[group])
            copy.start()
            kept.append(copy)
        for copy in kept:
            copy.wait()

    return pl.pallas_call(
        body,
        in_specs=[SM] + [ANY] * (count + 1),
        out_specs=ANY,
        out_shape=jax.ShapeDtypeStruct((parts, *shape), BF16),
        scratch_shapes=[
            pltpu.VMEM((height, length), BF16),
            pltpu.VMEM((length, depth), BF16),
            pltpu.VMEM((parts, *shape), BF16),
            pltpu.SemaphoreType.DMA,
            pltpu.SemaphoreType.DMA((2, count)),
            pltpu.SemaphoreType.DMA((2,)),
        ],
        compiler_params=params(),
        cost_estimate=cost(2 * height * length * depth, 20 * MIB, scale),
        name=name,
    )(jnp.zeros((8,), jnp.int32) if pos is None else pos, left, *arrays)


def rows_scratch(half, units, parts, cols):
    return [
        pltpu.VMEM((parts, units, cols), BF16),
        pltpu.VMEM((half, parts * cols), BF16),
        pltpu.SemaphoreType.DMA,
        pltpu.SemaphoreType.DMA((parts,)),
        pltpu.SemaphoreType.DMA((2,)),
    ]


def rows_of(left_copy, left, w_ref, units, o_ref, w_hold, made, w_sems, o_sems):
    parts, _, cols = w_ref.shape
    w_copies = [
        pltpu.make_async_copy(w_ref.at[part, pl.ds(0, units)], w_hold.at[part], w_sems.at[part])
        for part in range(parts)
    ]
    for copy in w_copies:
        copy.start()
    left_copy.wait()
    block = left()
    kept = []
    for group in range(2):
        members = range(group * parts // 2, (group + 1) * parts // 2)
        for part in members:
            w_copies[part].wait()
        for part in members:
            made[:, part * cols : (part + 1) * cols] = dot_nn(block, w_hold[part]).astype(BF16)
        columns = pl.ds(members.start * cols, len(members) * cols)
        copy = pltpu.make_async_copy(made.at[:, columns], o_ref.at[:, columns], o_sems.at[group])
        copy.start()
        kept.append(copy)
    for copy in kept:
        copy.wait()


def unit_rows(left, weight, core_step, name, scale=1):
    units, length = left.shape
    half = length // 2
    parts, _, cols = weight.shape

    def body(h_ref, w_ref, o_ref, held, w_hold, made, h_sem, w_sems, o_sems):
        h_copy = pltpu.make_async_copy(h_ref.at[:, pl.ds(core_step * half, half)], held, h_sem)
        h_copy.start()
        rows_of(h_copy, lambda: held[...].T, w_ref, units, o_ref, w_hold, made, w_sems, o_sems)

    return pl.pallas_call(
        body,
        in_specs=[ANY, ANY],
        out_specs=ANY,
        out_shape=jax.ShapeDtypeStruct((half, parts * cols), BF16),
        scratch_shapes=[pltpu.VMEM((units, half), BF16)]
        + rows_scratch(half, units, parts, cols),
        compiler_params=params(),
        cost_estimate=cost(2 * half * units * parts * cols, 9 * MIB, scale),
        name=name,
    )(left, weight)


def qkv_rows(pos, d_projected, weight, core_step, scale=1):
    tall, length = d_projected.shape
    rows = length // 8
    parts, _, cols = weight.shape

    def body(pos_ref, l_ref, w_ref, o_ref, held, w_hold, made, h_sem, w_sems, o_sems):
        for number in range(4):
            pltpu.make_async_copy(
                l_ref.at[:, chunk_lanes(pos_ref, 4 * core_step + number, rows)],
                held.at[:, pl.ds(number * rows, rows)],
                h_sem,
            ).start()
        h_copy = pltpu.make_async_copy(l_ref.at[:, pl.ds(0, 4 * rows)], held, h_sem)
        rows_of(h_copy, lambda: held[...].T, w_ref, tall, o_ref, w_hold, made, w_sems, o_sems)

    return pl.pallas_call(
        body,
        in_specs=[SM, ANY, ANY],
        out_specs=ANY,
        out_shape=jax.ShapeDtypeStruct((4 * rows, parts * cols), BF16),
        scratch_shapes=[pltpu.VMEM((tall, 4 * rows), BF16)]
        + rows_scratch(4 * rows, tall, parts, cols),
        compiler_params=params(),
        cost_estimate=cost(8 * rows * tall * parts * cols, 9 * MIB, scale),
        name="d_one_rows_sibling" if core_step else "d_one_rows_own",
    )(pos, d_projected, weight)


def chunk_lanes(pos_ref, chunk, rows):
    return pl.ds(pl.multiple_of(pos_ref[chunk] * rows, rows), rows)


def allowed_pairs(first_ref, q_at, k_at, size):
    lanes = pl.ds(pl.multiple_of(q_at * size, size), size)
    k_index = k_at * size + lax.broadcasted_iota(jnp.int32, (size, size), 0)
    q_index = q_at * size + lax.broadcasted_iota(jnp.int32, (size, size), 1)
    return (k_index >= first_ref[:, lanes]) & (k_index <= q_index)


def attend(pos, qkv, doc_first, start_block, size):
    length = qkv.shape[1]
    rows = length // 8
    width = qkv.shape[0] // 3
    heads = width // HEAD_DIM

    def body(pos_ref, start_ref, qkv_ref, first_ref, out_ref, log_ref, *refs):
        block_refs, held, acc = refs[:4], refs[4], refs[5]

        def query_block(q_at, _):
            q_lanes = pl.ds(pl.multiple_of(q_at * size, size), size)
            start = start_ref[q_at]
            every = range(heads)
            queries = [qkv_ref[h * HEAD_DIM : (h + 1) * HEAD_DIM, q_lanes] for h in every]

            def held_rows(k_at):
                return pl.ds(pl.multiple_of((k_at - start) * size, size), size)

            def find_top(k_at, tops):
                k_lanes = pl.ds(pl.multiple_of(k_at * size, size), size)
                mask = allowed_pairs(first_ref, q_at, k_at, size)
                new = []
                for head in every:
                    at = width + head * HEAD_DIM
                    logits = dot_tn(qkv_ref[at : at + HEAD_DIM, k_lanes], queries[head])
                    logits = jnp.where(mask, logits, -1e30)
                    held[head, held_rows(k_at), :] = logits
                    new.append(
                        jnp.maximum(
                            tops[head], jnp.max(logits.reshape(size // 8, 8, size), axis=0)
                        )
                    )
                return tuple(new)

            tops = lax.fori_loop(
                start,
                q_at + 1,
                find_top,
                tuple(jnp.full((8, size), -1e30, F32) for _ in every),
            )
            tops = [jnp.max(top, axis=0, keepdims=True) for top in tops]
            acc[...] = jnp.zeros_like(acc)

            def add_values(k_at, totals):
                k_lanes = pl.ds(pl.multiple_of(k_at * size, size), size)
                expons = []
                new = []
                for head in every:
                    expon = jnp.exp(held[head, held_rows(k_at), :] - tops[head])
                    new.append(
                        totals[head] + jnp.sum(expon.reshape(size // 8, 8, size), axis=0)
                    )
                    expons.append(expon.astype(BF16))
                outs = []
                for head in every:
                    at = 2 * width + head * HEAD_DIM
                    outs.append(dot_nn(qkv_ref[at : at + HEAD_DIM, k_lanes], expons[head]))
                acc[...] += jnp.concatenate(outs, axis=0)
                return tuple(new)

            totals = lax.fori_loop(
                start, q_at + 1, add_values, tuple(jnp.zeros((8, size), F32) for _ in every)
            )
            for head in every:
                total = jnp.sum(totals[head], axis=0, keepdims=True)
                band = slice(head * HEAD_DIM, (head + 1) * HEAD_DIM)
                out_ref[band, q_lanes] = (acc[band, :] / total).astype(BF16)
                log_ref[head : head + 1, q_lanes] = tops[head] + jnp.log(total)
            return 0

        lax.fori_loop(0, length // size, query_block, 0)
        for chunk in range(8):
            block = out_ref[:, chunk_lanes(pos_ref, chunk, rows)]
            block_refs[chunk % 4][chunk // 4] = block

    outs = pl.pallas_call(
        body,
        out_shape=[
            jax.ShapeDtypeStruct((width, length), BF16),
            jax.ShapeDtypeStruct((heads, length), F32),
        ]
        + [jax.ShapeDtypeStruct((2, width, rows), BF16)] * 4,
        in_specs=[SM, SM, VM, VM],
        out_specs=[VM] * 6,
        scratch_shapes=[
            pltpu.VMEM((heads, length, size), F32),
            pltpu.VMEM((width, size), F32),
        ],
        compiler_params=params(),
        cost_estimate=cost(0, 0),
        name="attend",
    )(pos, start_block, qkv, doc_first)
    return outs[0], outs[1], outs[2:]


def attend_back(
    pos, blocks, qkv, attended, log_sums, cosine, sine, doc_first, start_block, size
):
    width, length = attended.shape
    rows = length // 8
    heads = width // HEAD_DIM
    half_rot = ROT // 2
    scale = 1.0 / math.sqrt(HEAD_DIM)

    def body(pos_ref, start_ref, qkv_ref, att_ref, log_ref, c_ref, s_ref, first_ref, *refs):
        block_refs = refs[:5]
        out_ref, bias_ref, d_att, grads, sems = refs[5:]
        copies = exchanged_copies(
            block_refs, lambda chunk: d_att.at[:, chunk_lanes(pos_ref, chunk, rows)], sems
        )
        for copy in copies:
            copy.start()
        grads[...] = jnp.zeros_like(grads)
        for copy in copies:
            copy.wait()

        def query_block(q_at, _):
            q_lanes = pl.ds(pl.multiple_of(q_at * size, size), size)
            deltas = []
            for head in range(heads):
                at = head * HEAD_DIM
                deltas.append(
                    jnp.sum(
                        d_att[at : at + HEAD_DIM, q_lanes].astype(F32)
                        * att_ref[at : at + HEAD_DIM, q_lanes].astype(F32),
                        axis=0,
                        keepdims=True,
                    )
                )

            def key_block(k_at, _):
                k_lanes = pl.ds(pl.multiple_of(k_at * size, size), size)
                mask = allowed_pairs(first_ref, q_at, k_at, size)
                made = []
                for head in range(heads):
                    at = head * HEAD_DIM
                    key_at, value_at = width + at, 2 * width + at
                    query = qkv_ref[at : at + HEAD_DIM, q_lanes]
                    key = qkv_ref[key_at : key_at + HEAD_DIM, k_lanes]
                    value = qkv_ref[value_at : value_at + HEAD_DIM, k_lanes]
                    d_out = d_att[at : at + HEAD_DIM, q_lanes]
                    logits = dot_tn(key, query)
                    prob = jnp.where(
                        mask, jnp.exp(logits - log_ref[head : head + 1, q_lanes]), 0.0
                    )
                    d_prob = dot_tn(value, d_out)
                    d_logits = (prob * (d_prob - deltas[head])).astype(BF16)
                    made.append((query, key, d_out, d_logits, prob.astype(BF16)))
                for head in range(heads):
                    at = head * HEAD_DIM
                    key_at, value_at = width + at, 2 * width + at
                    query, key, d_out, d_logits, prob = made[head]
                    grads[at : at + HEAD_DIM, q_lanes] += dot_nn(key, d_logits)
                    grads[key_at : key_at + HEAD_DIM, k_lanes] += dot_nt(query, d_logits)
                    grads[value_at : value_at + HEAD_DIM, k_lanes] += dot_nt(d_out, prob)
                return 0

            lax.fori_loop(start_ref[q_at], q_at + 1, key_block, 0)
            return 0

        lax.fori_loop(0, length // size, query_block, 0)

        bias_ref[...] = jnp.zeros_like(bias_ref)

        def finish(at, _):
            lanes = pl.ds(pl.multiple_of(at * rows, rows), rows)
            cosines, sines = c_ref[:, lanes], s_ref[:, lanes]
            for kind in range(3):
                band = grads[kind * width : (kind + 1) * width, lanes]
                if kind == 0:
                    band = band * scale
                if kind < 2:
                    bands = []
                    for first in range(0, width, HEAD_DIM):
                        g_one = band[first : first + half_rot]
                        g_two = band[first + half_rot : first + ROT]
                        bands.append(g_one * cosines + g_two * sines)
                        bands.append(g_two * cosines - g_one * sines)
                        bands.append(band[first + ROT : first + HEAD_DIM])
                    band = jnp.concatenate(bands, axis=0)
                low = band.astype(BF16)
                out_ref[kind * width : (kind + 1) * width, lanes] = low
                bias_ref[kind * width : (kind + 1) * width, :] += jnp.sum(
                    low.astype(F32), axis=1, keepdims=True
                )
            return 0

        lax.fori_loop(0, length // rows, finish, 0)

    return pl.pallas_call(
        body,
        out_shape=[
            jax.ShapeDtypeStruct((3 * width, length), BF16),
            jax.ShapeDtypeStruct((3 * width, 1), F32),
        ],
        in_specs=[SM, SM] + [VM] * 6 + [ANY] * 5,
        out_specs=[VM, VM],
        scratch_shapes=[
            pltpu.VMEM((width, length), BF16),
            pltpu.VMEM((3 * width, length), F32),
            pltpu.SemaphoreType.DMA((8,)),
        ],
        compiler_params=params(),
        cost_estimate=cost(0, 0),
        name="attend_back",
    )(
        pos,
        start_block,
        qkv,
        attended,
        log_sums,
        cosine,
        sine,
        doc_first,
        *blocks,
    )


def doc_tables(doc_lengths, seq_length):
    doc_ends = jnp.cumsum(doc_lengths)
    doc_starts = doc_ends - doc_lengths
    places = jnp.arange(seq_length, dtype=jnp.int32)
    segment = jnp.sum((places[:, None] >= doc_ends[None, :-1]).astype(jnp.int32), axis=1)
    owners = segment[:, None] == jnp.arange(doc_lengths.shape[0], dtype=jnp.int32)[None, :]
    return places, jnp.sum(jnp.where(owners, doc_starts[None, :], 0), axis=1)


def shards(
    tokens,
    lengths,
    ln1_gain,
    ln1_bias,
    qkv_weight,
    qkv_bias,
    out_weight,
    ln2_gain,
    ln2_bias,
    gate_up_weight,
    down_weight,
    cotangent,
    axes,
):
    x = tokens[0]
    cot = cotangent[0]
    rows, depth = x.shape
    length = 8 * rows
    parts = axes["gx"]
    part_rows = depth // parts
    width = qkv_weight.shape[2]
    units = gate_up_weight.shape[2]
    size = 256
    gain_one = ln1_gain.astype(F32)[None]
    shift_one = ln1_bias.astype(F32)[None]
    gain_two = ln2_gain.astype(F32)[None]
    shift_two = ln2_bias.astype(F32)[None]

    attn_weight = jnp.concatenate(
        [qkv_weight.transpose(1, 2, 0).reshape(3 * width, part_rows), out_weight.T], axis=0
    )
    w_attn = lax.all_gather(attn_weight, "gx", axis=0, tiled=False)
    w_gate_up = lax.all_gather(
        gate_up_weight.transpose(1, 2, 0).reshape(2 * units, part_rows), "gx", axis=0, tiled=False
    )
    w_down = lax.all_gather(down_weight.T, "gx", axis=0, tiled=False)

    steps = jnp.arange(8, dtype=jnp.int32)
    pos = (lax.axis_index("gy") ^ (steps % 4)) * 2 + (lax.axis_index("gz") ^ (steps // 4))
    places, doc_first = doc_tables(lengths[0], length)
    start_block = doc_first[:: size] // size
    frequency = jnp.exp(
        jnp.arange(ROT // 2, dtype=F32) * (-2.0 * math.log(10000.0) / ROT)
    )
    angles = frequency[:, None] * (places - doc_first).astype(F32)[None, :]
    cosine, sine = jnp.cos(angles), jnp.sin(angles)
    doc_first = doc_first[None]

    bias_column = qkv_bias.astype(F32).reshape(3 * width, 1)
    normed_one = norm_one(x, gain_one, shift_one)
    one_pieces = gather_plane(normed_one, bias_column, cosine, sine, doc_first, start_block)
    cot_block = after(cot, one_pieces[1][0], one_pieces[2][0])
    cot_pieces = gather_plane(cot_block)
    out_block = w_attn[:, 3 * width :].transpose(1, 0, 2).reshape(width, depth)
    out_first = gather_first(out_block)
    qkv = project(
        pos,
        one_pieces,
        w_attn,
        after(bias_column, cot_pieces[3][0], cot_pieces[4][0], out_block),
        cosine,
        sine,
    )
    qkv = after(qkv, out_first[1], out_first[2], *[piece for piece, _, _ in cot_pieces])
    attended, log_sums, blocks = attend(pos, qkv, doc_first, start_block, size)
    exchanged = []

    def exchange(*arrived):
        got, other = exchange_plane(after(tuple(blocks), *arrived))
        exchanged.extend([*got, other])
        return exchanged[1:]

    out_pieces = gather_second(out_first, (qkv,), exchange)
    blocks = exchanged
    middle, normed_two = middle_norm(
        after(x, *[piece for piece, _, _ in cot_pieces]), blocks, out_pieces, gain_two, shift_two
    )

    two_pieces = gather_plane(normed_two)
    hidden, slopes = feed(two_pieces, w_gate_up)
    down_grad = grads_of(hidden, cot_pieces, parts, "down_grads", scale=0.1)
    down_grad_sum = lax.psum_scatter(down_grad, "gx", scatter_dimension=0, tiled=False)
    d_gate_up, d_two_sib = feed_back(cot_pieces, w_down, after(slopes, down_grad), w_gate_up, 1)
    d_gate_up, d_two_own = feed_back(
        cot_pieces, w_down, after(slopes, d_two_sib), w_gate_up, 0, d_gate_up
    )
    came, sent = scatter_first(d_two_own, d_two_sib, rows)
    gate_up_grad = grads_of(after(d_gate_up, *sent), two_pieces, parts, "gate_up_grads", scale=0.05)
    sent, arrived = scatter_second(d_two_own, came, sent, rows, gate_up_grad)
    gate_up_grad_sum = lax.psum_scatter(
        after(gate_up_grad, *sent), "gx", scatter_dimension=0, tiled=False
    )
    mlp_sib = unit_rows(
        after(hidden, gate_up_grad, *sent), w_down, 1, "mlp_rows_sibling", 0.1
    )
    d_two = scatter_last(d_two_own, came, sent, arrived)

    d_branch, norm_two_sums, d_middle, blocks = norm_two_back(
        after(middle, mlp_sib), cot, d_two, gain_two, out_pieces
    )
    got, other = exchange_plane(blocks)
    blocks = [*got, other]
    d_projected, bias_sums = attend_back(
        pos,
        blocks,
        qkv,
        after(attended, down_grad_sum),
        log_sums,
        cosine,
        sine,
        doc_first,
        start_block,
        size,
    )
    branch_pieces = gather_plane(after(d_branch, *blocks[1:]), d_projected)
    far_pieces = (branch_pieces[3][0], branch_pieces[4][0])
    qkv_grad = grads_of(
        after(d_projected, branch_pieces[1][0], branch_pieces[2][0]),
        one_pieces,
        parts,
        "qkv_grads",
        pos,
        kinds=3,
        scale=0,
    )
    qkv_grad = after(qkv_grad, *far_pieces)
    qkv_grad_sum = lax.psum_scatter(qkv_grad, "gx", scatter_dimension=0, tiled=False)
    d_one_sib = qkv_rows(pos, after(d_projected, qkv_grad), w_attn, 1, 0)
    d_one_own = qkv_rows(pos, after(d_projected, d_one_sib), w_attn, 0, 0)
    came, sent = scatter_first(d_one_own, d_one_sib, rows)
    out_grad = grads_of(
        after(attended, *sent), branch_pieces, parts, "out_grads", pos, kinds=1, scale=0
    )
    out_grad_sum = lax.psum_scatter(out_grad, "gx", scatter_dimension=0, tiled=False)
    mlp_own = unit_rows(after(hidden, out_grad), w_down, 0, "mlp_rows_own", 0)
    mlp_came, mlp_sent = scatter_first(mlp_own, after(mlp_sib, d_branch), rows)
    sent, arrived = scatter_second(d_one_own, came, sent, rows, *mlp_sent)
    d_one = scatter_last(d_one_own, came, sent, arrived)
    mlp_sent, mlp_arrived = scatter_second(mlp_own, mlp_came, after(mlp_sent, *sent), rows)

    mlp = scatter_last(mlp_own, mlp_came, mlp_sent, mlp_arrived)
    half = rows // 2
    total = mlp[0][:rows].astype(F32) + mlp[1][:rows].astype(F32)
    total = total + jnp.concatenate(
        [
            mlp[2][half:].astype(F32) + mlp[4].astype(F32),
            mlp[3].astype(F32) + mlp[5][half:].astype(F32),
        ],
        axis=0,
    )
    activations = (middle + total).astype(BF16)
    gate_up_grad_sum, down_grad_sum = after((gate_up_grad_sum, down_grad_sum), *sent)
    gate_up_out = gate_up_grad_sum.astype(F32).reshape(2, units, part_rows).transpose(2, 0, 1)
    down_out = down_grad_sum.astype(F32).T
    input_grad, norm_one_sums = norm_one_back(
        after(x, gate_up_out, down_out), d_middle, d_one, gain_one
    )

    bias_row = jnp.pad(bias_sums.reshape(1, 3 * width), ((0, 0), (0, depth - 3 * width)))
    small = jnp.concatenate([norm_one_sums, norm_two_sums, bias_row], axis=0)
    small = sum_all(small, [("gx", axes["gx"])])
    bias_sum = small[4, : 3 * width].reshape(3, width)
    norm_sums = sum_all(small[:4], [("gz", axes["gz"]), ("gy", axes["gy"])])
    qkv_grad_sum, out_grad_sum = after(
        (qkv_grad_sum, out_grad_sum[0]), activations, norm_sums, bias_sum, gate_up_out, down_out
    )
    return (
        activations[None],
        input_grad[None],
        norm_sums[0],
        norm_sums[1],
        qkv_grad_sum.astype(F32).transpose(1, 0, 2),
        bias_sum,
        out_grad_sum.astype(F32),
        norm_sums[2],
        norm_sums[3],
        gate_up_out,
        down_out,
    )


def solution(mesh):
    axes = dict(mesh.shape)
    placed = (
        P("gx", ("gy", "gz"), None),
        P("gx", None),
        P(),
        P(),
        P("gx", None, ("gy", "gz")),
        P(None, ("gy", "gz")),
        P("gx", ("gy", "gz")),
        P(),
        P(),
        P("gx", None, ("gy", "gz")),
        P("gx", ("gy", "gz")),
        P("gx", ("gy", "gz"), None),
    )
    return jax.shard_map(
        lambda *args: shards(*args, axes),
        mesh=mesh,
        in_specs=placed,
        out_specs=(
            P("gx", ("gy", "gz"), None),
            P("gx", ("gy", "gz"), None),
            P(),
            P(),
            P("gx", None, ("gy", "gz")),
            P(None, ("gy", "gz")),
            P("gx", ("gy", "gz")),
            P(),
            P(),
            P("gx", None, ("gy", "gz")),
            P("gx", ("gy", "gz")),
        ),
        check_vma=False,
    )
```
